128 devices in a mesh: rep: 32 (over x, z, core), tp: 4 (over y).
Axes of the slice: x: 4, y: 4, z: 4, core: 2. Of those that a mesh axis runs over, the one named last changes fastest.
Arguments:
- query: bfloat16 [1024, 4096], P('rep', 'tp'), may hold values from -8 to 8
- kv_pool: bfloat16 [2, 4, 8192, 64, 128], P(None, 'tp', 'rep'), may hold values from -6 to 6
- page_table: int32 [1024, 8], P('rep'), may hold values from 0 to 255, as said below
- lengths: int32 [1024], P('rep'), may hold values from 1 to 512, 262144 in all
- residual: bfloat16 [1024, 4096], P('rep'), may hold values from -64 to 64
- w_out: bfloat16 [4096, 4096], P('tp'), may hold values from -0.09375 to 0.09375
- norm_gain: bfloat16 [4096], replicated, may hold values from 0.099609375 to 1.8984375
- route_ids: int32 [1024, 8], P('rep'), may hold values from 0 to 31, all different within a row; in each aligned block of 32 rows (0 to 31, 32 to 63, ...) at most 16 rows name the same one
- route_weights: float32 [1024, 8], P('rep'), may hold values from 0.05 to 1
- w_gate: bfloat16 [32, 4096, 1536], P('rep', None, 'tp'), may hold values from -0.09375 to 0.09375
- w_up: bfloat16 [32, 4096, 1536], P('rep', None, 'tp'), may hold values from -0.09375 to 0.09375
- w_down: bfloat16 [32, 1536, 4096], P('rep', 'tp'), may hold values from -0.15625 to 0.15625
Outputs:
- layer_out: bfloat16 [1024, 4096], P('rep', 'tp')
The draws below stay inside these ranges and needn't reach their ends.
Inputs may be any that keep to these rules, and one draw needn't show every extreme that they name: `page_table`: each replica's 32 rows hold distinct pages of that replica's pool, and together all of them. `route_ids`: within the 32 rows of one replica no expert is named by more than 16 rows; a row names 8 different experts.
All inputs are finite; a program needn't handle non-finite values. No bound on the sum of `lengths` on one device may be relied on, other than what follows from the above.
Results may differ from the reference program's by a relative error of at most 0.0035.
Values may be sent and summed in bfloat16 or wider, within the bound.
A program may use at most 128 MiB of HBM per device.

```python
import math
import jax
import jax.numpy as jnp
import numpy as np
from jax import lax

D = 4096
KVH = 4
HD = 128
FF = 1536
TOPK = 8
QH = 32
PAGE = 64
ROWS_REP = 32
CTX = 512
EXPERTS = 32
CAP = 16
MAXP = 8
PAGES_REP = 256
POOL = 8192
ROWS = 1024
N_REP = 32


def draw_query(key, part):
    key = jax.random.fold_in(key, 1)
    values = jnp.clip(jax.random.normal(key, (ROWS, QH * HD), jnp.float32), -6.0, 6.0)
    return values.astype(jnp.bfloat16)


def draw_kv_pool(key, part):
    key = jax.random.fold_in(key, 2)
    values = jnp.clip(jax.random.normal(key, (2, KVH, POOL, PAGE, HD), jnp.float32), -6.0, 6.0)
    return values.astype(jnp.bfloat16)


def draw_page_table(key, part):
    key = jax.random.fold_in(key, 3)
    replica_keys = jax.random.split(key, N_REP)
    orders = jax.vmap(lambda one_key: jax.random.permutation(one_key, PAGES_REP))(replica_keys)
    return orders.reshape(ROWS, MAXP).astype(jnp.int32)


def draw_residual(key, part):
    key = jax.random.fold_in(key, 4)
    key_cols, key_rows, key_vals = jax.random.split(key, 3)
    ramp = 1.0 + 2.0 * jnp.arange(D, dtype=jnp.float32) / (D - 1)
    col_scale = ramp * jnp.exp(jax.random.uniform(key_cols, (D,), jnp.float32, 0.0, math.log(3.5)))
    row_scale = 0.15 * jnp.exp(jax.random.uniform(key_rows, (ROWS, 1), jnp.float32, 0.0, math.log(10.0)))
    base_draw = jnp.clip(jax.random.normal(key_vals, (ROWS, D), jnp.float32), -3.5, 3.5)
    return (base_draw * col_scale[None, :] * row_scale).astype(jnp.bfloat16)


def block_levels(key, shape, cuts, low, top_value):
    loudness, own = 1.0, jax.random.fold_in(key, 6)
    for dim, parts in cuts:
        steps = jnp.exp(jax.random.uniform(jax.random.fold_in(own, dim), (parts,), jnp.float32, low / len(cuts), top_value / len(cuts)))
        loudness = loudness * jnp.repeat(steps, shape[dim] // parts).reshape([-1 if axis == dim else 1 for axis in range(len(shape))])
    return loudness


def profile(count, total, limit, skew):
    loads = [(1 << 20) // math.isqrt(grade ** skew) + 1 for grade in range(2, count + 1)]
    spare, counts = total - limit - (count - 1), [1] * (count - 1)
    while spare > 0:
        movable = [i for i in range(count - 1) if counts[i] < limit]
        mass, budget = sum([loads[i] for i in movable]), spare
        for i in movable:
            addition = min(limit - counts[i], max(1, budget * loads[i] // mass), spare)
            counts[i] = counts[i] + addition
            spare = spare - addition
    return np.array([limit] + counts)


def ragged_sizes(key, amount, total, reach, slope):
    if amount == 2:
        one = jax.random.randint(key, (), max(1, total - reach), min(reach, total - 1) + 1)
        return jnp.stack([one, total - one])
    sizes = jnp.asarray(profile(amount, total, reach, slope), jnp.int32)
    pairs = (amount - 1) // 2
    donor, sink = sizes[1:1 + 2 * pairs:2], sizes[2:2 + 2 * pairs:2]
    margin = jnp.minimum(donor - 1, reach - sink)
    moved = jax.random.randint(jax.random.fold_in(key, 1), (pairs,), 0, 1 << 20) % (margin + 1)
    sizes = sizes.at[1:1 + 2 * pairs:2].set(donor - moved).at[2:2 + 2 * pairs:2].set(sink + moved)
    return sizes[jax.random.permutation(jax.random.fold_in(key, 2), amount)]


def shared_out(own_key, own, number, rows, number_of, top, reach, slope):
    sequence = jax.random.permutation(own_key, number_of)
    crowded, common = shares(number_of, rows * top, reach, slope, True), shares(number_of, rows * top, reach, slope, False)
    places = jnp.arange(number_of)

    def named(tallies, turn):
        used = int((tallies > 0).sum())
        fixed = max(1, used // 4)
        passed = fixed + (places - fixed + turn * (used - fixed)) % max(1, number_of - fixed)
        return jnp.zeros((number_of,), jnp.int32).at[sequence[jnp.where(places < fixed, places, passed)]].set(jnp.asarray(tallies, jnp.int32))

    tallies = jnp.where(number % 4 == 0, named(crowded, number // 4), named(common, number - number // 4 - 1))
    mixed = jax.random.permutation(jax.random.fold_in(own, 3), number_of)
    source_of, taker = mixed[0:number_of // 2 * 2:2], mixed[1:number_of // 2 * 2:2]
    margin = jnp.minimum(tallies[source_of] - 1, reach - tallies[taker]) // 2
    margin = jnp.where((source_of == sequence[0]) | (taker == sequence[0]) | (tallies[taker] == 0), 0, jnp.maximum(margin, 0))
    passed = jax.random.randint(jax.random.fold_in(own, 4), (number_of // 2,), 0, 1 << 20) % (margin + 1)
    tallies = tallies.at[source_of].add(-passed).at[taker].add(passed)
    members = jnp.searchsorted(jnp.cumsum(tallies), jnp.arange(rows * top), side="right").astype(jnp.int32)
    table = members.reshape(top, rows).T
    table = table[jax.random.permutation(jax.random.fold_in(own, 1), rows)]
    turn = jax.random.randint(jax.random.fold_in(own, 2), (rows, 1), 0, top)
    return jnp.take_along_axis(table, (jnp.arange(top)[None, :] + turn) % top, axis=1)


def shares(amount, total, most, lean, full):
    weights = [(1 << 20) // math.isqrt(rank ** lean) + 1 for rank in range(1, amount + 1)]
    largest = most if full else min(most, max(-(-total // amount), total * weights[0] // sum(weights)))
    least = 1 if total - largest >= amount - 1 else 0
    counts, rest = [largest] + [least] * (amount - 1), total - largest - least * (amount - 1)
    while rest > 0:
        candidates = [i for i in range(1, amount) if counts[i] < largest] or [i for i in range(1, amount) if counts[i] < most]
        mass, budget = sum([weights[i] for i in candidates]), rest
        for i in candidates:
            extra = min(most - counts[i], max(1, budget * weights[i] // mass), rest)
            counts[i] = counts[i] + extra
            rest = rest - extra
    return np.array(counts)


def scatter_about(rng, shape, scale, most, cuts=(), kind=jnp.bfloat16):
    factor_of = block_levels(rng, shape, cuts, -0.22, 0.18) if cuts else 1.0
    entries = jax.random.normal(rng, shape, jnp.float32) * scale * factor_of
    return jnp.minimum(jnp.maximum(entries, -most), most).astype(kind)


def setup_inputs(seed: int = 0) -> dict:
    seeds = jax.random.split(jax.random.key(seed), 13)
    query = draw_query(jax.random.fold_in(seeds[12], 71), 0)
    kv_pool = draw_kv_pool(jax.random.fold_in(seeds[12], 71), 0)
    page_table = draw_page_table(jax.random.fold_in(seeds[12], 71), 0)
    lengths = ragged_sizes(seeds[3], ROWS, ROWS * CTX // 2, CTX, 2).astype(jnp.int32)
    residual = draw_residual(jax.random.fold_in(seeds[12], 71), 0)
    w_out = scatter_about(seeds[5], (QH * HD, D), (QH * HD) ** -0.5, 0.09375, ((0, 4),))
    norm_gain = jnp.clip(1.0 + 0.18 * jax.random.normal(seeds[6], (D,), jnp.float32), 0.099609375, 1.8984375).astype(jnp.bfloat16)
    route_ids_keys = jax.random.split(jax.random.fold_in(seeds[7], 1), ROWS // ROWS_REP)
    route_ids_turns = jax.random.permutation(jax.random.fold_in(seeds[7], 3), ROWS // ROWS_REP)
    route_ids = jax.vmap(lambda own, number: shared_out(jax.random.fold_in(seeds[7], 2), own, number, ROWS_REP, EXPERTS, TOPK, CAP, 2))(route_ids_keys, route_ids_turns).reshape((ROWS, TOPK))
    route_weights = jnp.clip(0.05 + 0.95 * jax.random.uniform(seeds[8], (ROWS, TOPK), jnp.float32) ** block_levels(seeds[8], (ROWS, TOPK), ((0, 32),), -0.2, 0.2), 0.05, 1.0)
    w_gate = scatter_about(seeds[9], (EXPERTS, D, FF), D ** -0.5, 0.09375, ((0, 32), (2, 4)))
    w_up = scatter_about(seeds[10], (EXPERTS, D, FF), D ** -0.5, 0.09375, ((0, 32), (2, 4)))
    w_down = scatter_about(seeds[11], (EXPERTS, FF, D), FF ** -0.5, 0.15625, ((0, 32), (1, 4)))
    return dict(query=query, kv_pool=kv_pool, page_table=page_table, lengths=lengths, residual=residual, w_out=w_out, norm_gain=norm_gain, route_ids=route_ids, route_weights=route_weights, w_gate=w_gate, w_up=w_up, w_down=w_down)


norm_epsilon = 1e-06

def reference(query, kv_pool, page_table, lengths, residual, w_out, norm_gain, route_ids, route_weights, w_gate, w_up, w_down):
    group_size = QH // KVH
    score_scale = HD ** (-0.5)

    def one_replica(replica):
        first = replica * ROWS_REP
        queries = lax.dynamic_slice_in_dim(query, first, ROWS_REP, 0).astype(jnp.float32)
        queries = queries.reshape(ROWS_REP, KVH, group_size, HD)
        table = lax.dynamic_slice_in_dim(page_table, first, ROWS_REP, 0) + replica * PAGES_REP
        row_lengths = lax.dynamic_slice_in_dim(lengths, first, ROWS_REP, 0)
        page_rows = jnp.take(kv_pool, table.reshape(-1), axis=2)
        page_rows = page_rows.reshape(2, KVH, ROWS_REP, CTX, HD).astype(jnp.float32)
        scores = jnp.einsum('rkgd,krcd->rkgc', queries, page_rows[0]) * score_scale
        valid_keys = jnp.arange(CTX, dtype=jnp.int32)[None, :] < row_lengths[:, None]
        scores = jnp.where(valid_keys[:, None, None, :], scores, -1e+30)
        top_score = lax.optimization_barrier(jnp.max(scores, axis=-1, keepdims=True))
        weights = jnp.exp(scores - top_score)
        probs = (weights / lax.optimization_barrier(jnp.sum(weights, axis=-1, keepdims=True))).astype(jnp.bfloat16)
        probs = lax.optimization_barrier(probs).astype(jnp.float32)
        mixed = jnp.einsum('rkgc,krcd->rkgd', probs, page_rows[1])
        return mixed.reshape(ROWS_REP, QH * HD).astype(jnp.bfloat16)
    attn = lax.map(one_replica, jnp.arange(N_REP, dtype=jnp.int32)).reshape(ROWS, QH * HD)
    hidden = residual.astype(jnp.float32) + jnp.dot(attn, w_out, preferred_element_type=jnp.float32)
    mean_square = lax.optimization_barrier(jnp.mean(hidden * hidden, axis=-1, keepdims=True))
    normed = (hidden * lax.rsqrt(mean_square + norm_epsilon) * norm_gain.astype(jnp.float32)).astype(jnp.bfloat16)
    flat_ids = route_ids.reshape(N_REP, ROWS_REP * TOPK)
    expert_iota = jnp.arange(EXPERTS, dtype=jnp.int32)
    onehot = (flat_ids[:, :, None] == expert_iota[None, None, :]).astype(jnp.int32)
    earlier = (jnp.cumsum(onehot, axis=1) - onehot).astype(jnp.int32)
    slot_index = lax.optimization_barrier(jnp.sum(earlier * onehot, axis=-1)).astype(jnp.int32)
    target = (flat_ids * CAP + slot_index).astype(jnp.int32)
    row_of = (jnp.arange(ROWS_REP * TOPK, dtype=jnp.int32) // TOPK).astype(jnp.int32)
    source = jnp.full((N_REP, EXPERTS * CAP), ROWS_REP, jnp.int32)
    source = source.at[jnp.arange(N_REP, dtype=jnp.int32)[:, None], target].set(jnp.broadcast_to(row_of[None, :], target.shape))
    normed_pad = jnp.concatenate([normed.reshape(N_REP, ROWS_REP, D), jnp.zeros((N_REP, 1, D), jnp.bfloat16)], axis=1)
    inputs = jnp.take_along_axis(normed_pad, source[:, :, None], axis=1)
    inputs = inputs.reshape(N_REP, EXPERTS, CAP, D).transpose(1, 0, 2, 3).reshape(EXPERTS, N_REP * CAP, D)

    def one_expert(expert_args):
        rows_in, gate_weight, up_weight, down_weight = expert_args
        gate = jnp.dot(rows_in, gate_weight, preferred_element_type=jnp.float32)
        upward = jnp.dot(rows_in, up_weight, preferred_element_type=jnp.float32)
        act = (jax.nn.silu(gate) * upward).astype(jnp.bfloat16)
        return jnp.dot(act, down_weight, preferred_element_type=jnp.float32).astype(jnp.bfloat16)
    outputs = lax.map(one_expert, (inputs, w_gate, w_up, w_down))
    back = outputs.reshape(EXPERTS, N_REP, CAP, D).transpose(1, 0, 2, 3).reshape(N_REP, EXPERTS * CAP, D)
    picked = jnp.take_along_axis(back, target[:, :, None], axis=1).reshape(ROWS, TOPK, D).astype(jnp.float32)
    moe = lax.optimization_barrier(jnp.sum(route_weights[:, :, None] * picked, axis=1))
    return (hidden + moe).astype(jnp.bfloat16)
```

```python
import jax
import jax.numpy as jnp
from jax import lax
from jax.sharding import PartitionSpec as P

norm_epsilon = 1e-06


def local(
    query,
    kv_pool,
    page_table,
    lengths,
    residual,
    w_out,
    norm_gain,
    route_ids,
    route_weights,
    w_gate,
    w_up,
    w_down,
):
    row_count = query.shape[0]
    kv_local = kv_pool.shape[1]
    page_len = kv_pool.shape[3]
    head_dim = kv_pool.shape[4]
    group_size = query.shape[1] // (kv_local * head_dim)
    context = page_table.shape[1] * page_len
    feature_count = residual.shape[1]
    share_width = feature_count // lax.axis_size("tp")
    tp_pos = lax.axis_index("tp")
    rep_pos = lax.axis_index("rep")
    owner_count = lax.axis_size("rep")
    top_count = route_ids.shape[1]
    expert_iota = jnp.arange(owner_count, dtype=jnp.int32)
    onehot = route_ids[:, :, None] == expert_iota[None, None, :]
    spread = jnp.sum(jnp.where(onehot, route_weights[:, :, None], 0.0), axis=1)
    spread_all = lax.all_gather(spread, "rep", axis=0, tiled=True)
    own_weight = lax.dynamic_slice_in_dim(spread_all, rep_pos, 1, 1)

    cache = jnp.take(kv_pool, page_table.reshape(-1), axis=2)
    cache = cache.reshape(2, kv_local, row_count, context, head_dim)
    queries = query.reshape(row_count, kv_local, group_size, head_dim)
    scores = jnp.einsum("rkgd,krcd->rkgc", queries, cache[0], preferred_element_type=jnp.float32)
    scores = scores * head_dim ** (-0.5)
    valid_keys = jnp.arange(context, dtype=jnp.int32)[None, :] < lengths[:, None]
    scores = jnp.where(valid_keys[:, None, None, :], scores, -1e30)
    top_score = jnp.max(scores, axis=-1, keepdims=True)
    weights = jnp.exp(scores - top_score)
    probs = (weights / jnp.sum(weights, axis=-1, keepdims=True)).astype(jnp.bfloat16)
    mixed = jnp.einsum("rkgc,krcd->rkgd", probs, cache[1], preferred_element_type=jnp.float32)
    attn = mixed.reshape(row_count, kv_local * group_size * head_dim).astype(jnp.bfloat16)
    partial_out = jnp.dot(attn, w_out, preferred_element_type=jnp.float32)
    attn_share = lax.psum_scatter(partial_out, "tp", scatter_dimension=1, tiled=True)
    residual_share = lax.dynamic_slice_in_dim(residual, tp_pos * share_width, share_width, 1)
    gain_share = lax.dynamic_slice_in_dim(norm_gain, tp_pos * share_width, share_width, 0)
    hidden = residual_share.astype(jnp.float32) + attn_share
    square_sum = lax.psum(jnp.sum(hidden * hidden, axis=-1, keepdims=True), "tp")
    mean_square = square_sum / feature_count
    normed = (
        hidden * lax.rsqrt(mean_square + norm_epsilon) * gain_share.astype(jnp.float32)
    ).astype(jnp.bfloat16)
    rows = lax.all_gather(normed, "tp", axis=1, tiled=True)
    rows = lax.all_gather(rows, "rep", axis=0, tiled=True)
    gate = jnp.dot(rows, w_gate[0], preferred_element_type=jnp.float32)
    upward = jnp.dot(rows, w_up[0], preferred_element_type=jnp.float32)
    act = (jax.nn.silu(gate) * upward).astype(jnp.bfloat16)
    expert_terms = jnp.dot(act, w_down[0], preferred_element_type=jnp.float32)
    expert_terms = (expert_terms * own_weight).astype(jnp.bfloat16)
    moe = lax.psum_scatter(expert_terms, "tp", scatter_dimension=1, tiled=True)
    moe = lax.psum_scatter(moe, "rep", scatter_dimension=0, tiled=True)
    return (hidden + moe.astype(jnp.float32)).astype(jnp.bfloat16)


def solution(mesh):
    in_specs = (
        P("rep", "tp"),
        P(None, "tp", "rep", None, None),
        P("rep", None),
        P("rep"),
        P("rep", None),
        P("tp", None),
        P(),
        P("rep", None),
        P("rep", None),
        P("rep", None, "tp"),
        P("rep", None, "tp"),
        P("rep", "tp", None),
    )
    out_specs = P("rep", "tp")
    return jax.shard_map(local, mesh=mesh, in_specs=in_specs, out_specs=out_specs, check_vma=False)
```

```python
import functools

import jax
import jax.numpy as jnp
from jax import lax
from jax.experimental import pallas as pl
from jax.experimental.pallas import tpu as pltpu
from jax.sharding import PartitionSpec as P

norm_epsilon = 1e-06
MESH = pl.DeviceIdType.MESH
BF, F32 = jnp.bfloat16, jnp.float32
RING = 4
ROWS = 32
SHARE = 1024
HIDDEN = 384
ORDER = (("x", "y", "z"), ("y", "z", "x"), ("z", "x", "y"))
START = (0, 384, 768)
WIDE = (384, 384, 256)
CARRY = 384


def experts_kernel(
    part, residual, gain, ids, weights, w_gate, w_up, w_down, out,
    w_in, w_back, g0, g1, g2, acc, act, row_weight, hidden,
    p_in, sq_out, sq_in, y0, y1, y2, s0, s1, s2, l0, l1, l2, f0, f1, f2,
    t0, t1, t2, m0, m1, m2, u0, u1, u2, n0, n1, n2,
    send_sem, recv_sem, load_sem,
):
    rep, y = lax.axis_index("rep"), lax.axis_index("tp")
    x, z, core = rep // 8, (rep // 2) % 4, rep % 2
    at = {"x": x, "y": y, "z": z}
    G, Y, S = (g0, g1, g2), (y0, y1, y2), (s0, s1, s2)
    L, F, T, M, U, N = (l0, l1, l2), (f0, f1, f2), (t0, t1, t2), (m0, m1, m2), (u0, u1, u2), (n0, n1, n2)

    def near(axis, off):
        return lax.rem(at[axis] + off, RING)

    def peer(axis, off):
        c = dict(at)
        c[axis] = near(axis, off)
        return ((c["x"] * RING + c["z"]) * 2 + core, c["y"])

    twin = ((x * RING + z) * 2 + 1 - core, y)

    barrier = pltpu.get_barrier_semaphore()
    others = [peer(a, o) for a in "xyz" for o in (1, 2, 3)] + [twin]
    for other in others:
        pl.semaphore_signal(barrier, inc=1, device_id=other, device_id_type=MESH)

    loads = []
    for i, (src, dst) in enumerate((
        (w_gate.at[0], w_in.at[:, pl.ds(0, HIDDEN)]),
        (w_up.at[0], w_in.at[:, pl.ds(HIDDEN, HIDDEN)]),
        (w_down.at[0], w_back),
    )):
        load = pltpu.make_async_copy(src, dst, load_sem.at[i])
        load.start()
        loads.append(load)

    sends = []

    def send(src, dst, to):
        i = len(sends)
        copy = pltpu.make_async_remote_copy(
            src_ref=src, dst_ref=dst, send_sem=send_sem.at[i], recv_sem=recv_sem.at[i],
            device_id=to, device_id_type=MESH,
        )
        copy.start()
        sends.append(copy)
        return i

    def arrived(i, landing):
        pltpu.make_async_remote_copy(
            src_ref=landing, dst_ref=landing, send_sem=send_sem.at[i], recv_sem=recv_sem.at[i],
            device_id=twin, device_id_type=MESH,
        ).wait_recv()

    lane = lax.broadcasted_iota(jnp.int32, (ROWS, 128), 1)
    spread = jnp.zeros((ROWS, 128), F32)
    for k in range(8):
        spread = spread + jnp.where(lane % 32 == ids[:, k : k + 1], weights[:, k : k + 1], 0.0)
    top = spread.astype(BF).astype(F32)
    mid = (spread - top).astype(BF).astype(F32)
    low = spread - top - mid
    third = lane // 32
    spread = jnp.where(third == 0, top, jnp.where(third == 1, mid, jnp.where(third == 2, low, 0.0)))

    pl.semaphore_wait(barrier, len(others))

    ids_p = {}
    for o in (2, 1, 3):
        ids_p[o] = send(part.at[near("y", o)], p_in.at[o - 1], peer("y", o))
    acc[...] = jnp.zeros_like(acc)
    col = pl.ds(pl.multiple_of(y * SHARE, SHARE), SHARE)
    total = residual[:, col].astype(F32) + part[y].astype(F32)
    for o in (1, 3, 2):
        arrived(ids_p[o], p_in.at[o - 1])
        total = total + p_in[o - 1].astype(F32)
    hidden[...] = total
    square = jnp.sum(total * total, axis=1, keepdims=True)
    sq_out[...] = jnp.broadcast_to(square, (ROWS, 128))
    ids_q = {o: send(sq_out, sq_in.at[o - 1], peer("y", o)) for o in (2, 1, 3)}
    scaled_gain = gain[:, col].astype(F32)
    square = sq_out[...]
    for o in (1, 3, 2):
        arrived(ids_q[o], sq_in.at[o - 1])
        square = square + sq_in[o - 1]
    scale = lax.rsqrt(square[:, 0:1] * (1.0 / (RING * SHARE)) + norm_epsilon)
    normed = (hidden[...] * scale * scaled_gain).astype(BF)

    def block(p, i3, i2, first, count, c):
        inner = pl.ds(first, count)
        if p == 1:
            return G[p].at[i3, inner, i2, c]
        return G[p].at[i3, i2, inner, c]

    own = [tuple(at[a] for a in ORDER[p]) for p in range(3)]
    mine = (g0.at[z, y, x, core], g1.at[x, y, z, core], g2.at[y, x, z, core])
    for p in range(3):
        piece = normed[:, START[p] : START[p] + WIDE[p]]
        if WIDE[p] < CARRY:
            piece = jnp.concatenate([piece, spread.astype(BF)], axis=1)
        mine[p][...] = piece

    one = [{} for _ in range(3)]
    two = [{} for _ in range(3)]
    plain = [{} for _ in range(3)]
    relay = [{} for _ in range(3)]
    across = [{} for _ in range(3)]

    def to_twin(p, i3, i2, key):
        ref = block(p, i3, i2, 0, RING, core)
        across[p][key] = send(ref, ref, twin)

    def send_plain(p, s):
        q1, q2, q3 = own[p]
        ref = block(p, q3, near(ORDER[p][1], (4 - s) % 4), 0, RING, core)
        for o in (1, 3):
            plain[p][s, o] = send(ref, ref, peer(ORDER[p][2], o))
        to_twin(p, q3, near(ORDER[p][1], (4 - s) % 4), (0, s))

    for p in range(3):
        q1, q2, q3 = own[p]
        ref = block(p, q3, q2, q1, 1, core)
        for o in (1, 3, 2):
            one[p][o] = send(ref, ref, peer(ORDER[p][0], o))
    for p in range(3):
        q1, q2, q3 = own[p]
        for o in (1, 3, 2):
            arrived(one[p][o], block(p, q3, q2, near(ORDER[p][0], 4 - o), 1, core))
        ref = block(p, q3, q2, 0, RING, core)
        for o in (1, 3, 2):
            two[p][o] = send(ref, ref, peer(ORDER[p][1], o))
        send_plain(p, 0)
    for o in (1, 3, 2):
        for p in range(3):
            q1, q2, q3 = own[p]
            arrived(two[p][o], block(p, q3, near(ORDER[p][1], 4 - o), 0, RING, core))
            send_plain(p, o)

    def pass_on(s):
        for p in range(3):
            i2 = near(ORDER[p][1], (4 - s) % 4)
            for o in (1, 3):
                i3 = near(ORDER[p][2], 4 - o)
                arrived(plain[p][s, o], block(p, i3, i2, 0, RING, core))
                ref = block(p, i3, i2, 0 if o == 1 else 2, 2, core)
                relay[p][s, o] = send(ref, ref, peer(ORDER[p][2], o))
                to_twin(p, i3, i2, (o, s))

    def last_in(s):
        for p in range(3):
            i2 = near(ORDER[p][1], (4 - s) % 4)
            i3 = near(ORDER[p][2], 2)
            arrived(relay[p][s, 1], block(p, i3, i2, 0, 2, core))
            arrived(relay[p][s, 3], block(p, i3, i2, 2, 2, core))
            to_twin(p, i3, i2, (2, s))

    def twin_in(p, d):
        i3 = near(ORDER[p][2], (4 - d) % 4)
        for s in (0, 1, 3, 2):
            i2 = near(ORDER[p][1], (4 - s) % 4)
            arrived(across[p][d, s], block(p, i3, i2, 0, RING, 1 - core))
        return i3

    def project(p, d):
        i3 = twin_in(p, d)
        width = WIDE[p]

        def columns(n, _):
            c = pl.ds(pl.multiple_of(n * 256, 256), 256)
            if p == 2:
                w = w_in[pl.ds(pl.multiple_of(i3 * SHARE + START[2], 256), width), c]
                for i in range(RING):
                    rows = g2[i3, i, :, :, :, 0:width].reshape(256, width)
                    acc[i, :, :, c] += jnp.dot(rows, w, preferred_element_type=F32).reshape(RING, 64, 256)
                return 0
            total = jnp.zeros((256, 256), F32)
            for t in range(RING):
                rows = G[p][i3, t].reshape(256, width)
                w = w_in[t * SHARE + START[p] : t * SHARE + START[p] + width, c]
                total = total + jnp.dot(rows, w, preferred_element_type=F32)
            total = total.reshape(RING, 64, 256)
            if p == 0:
                acc[:, i3, :, c] += total
            else:
                acc[i3, :, :, c] += total
            return 0

        lax.fori_loop(0, 3, columns, 0)

    pass_on(0)
    loads[0].wait()
    loads[1].wait()
    project(0, 0)
    pass_on(1)
    project(1, 0)
    pass_on(3)
    project(2, 0)
    pass_on(2)
    last_in(0)
    project(0, 1)
    project(1, 1)
    last_in(1)
    project(2, 1)
    project(0, 3)
    last_in(3)
    project(1, 3)
    project(2, 3)
    last_in(2)
    for p in range(3):
        project(p, 2)

    pick = lax.broadcasted_iota(jnp.int32, (128, 128), 0)
    pick = jnp.where((pick % 32 == rep) & (pick < 96), 1.0, 0.0).astype(BF)

    def units(i, _):
        table = g2[y, i, :, :, :, 256:384].reshape(256, 128)
        row_weight[i] = jnp.dot(table, pick, preferred_element_type=F32).reshape(RING, 64, 128)
        g = acc[i, :, :, 0:HIDDEN]
        u = acc[i, :, :, HIDDEN : 2 * HIDDEN]
        act[i] = (g / (1.0 + jnp.exp(-g)) * u).astype(BF)
        return 0

    lax.fori_loop(0, RING, units, 0)
    loads[2].wait()

    def sub(p, ref, i2, first, count):
        inner = pl.ds(first, count)
        if p == 1:
            return ref.at[inner, i2]
        return ref.at[i2, inner]

    def weighted(value, w, width):
        return jnp.concatenate(
            [value[:, j * 128 : (j + 1) * 128] * w for j in range(width // 128)], axis=1
        ).astype(BF)

    crossed = [{} for _ in range(3)]

    def back(p, d):
        i3 = near(ORDER[p][2], d)
        width = WIDE[p]
        if p == 2:
            w = w_back[:, pl.ds(pl.multiple_of(i3 * SHARE + START[2], 256), width)]

            def body(i, _):
                value = jnp.dot(act[i].reshape(256, HIDDEN), w, preferred_element_type=F32)
                value = weighted(value, row_weight[i].reshape(256, 128), width).reshape(RING, 2, ROWS, width)
                for k in range(2):
                    y2[k, i3, i] = value[:, k]
                return 0

            lax.fori_loop(0, RING, body, 0)
        else:
            if p == 0:
                a = act[:, i3].reshape(256, HIDDEN)
                rw = row_weight[:, i3].reshape(256, 128)
            else:
                a = act[i3].reshape(256, HIDDEN)
                rw = row_weight[i3].reshape(256, 128)

            def body(t, _):
                w = w_back[:, pl.ds(pl.multiple_of(t * SHARE + START[p], 128), width)]
                value = jnp.dot(a, w, preferred_element_type=F32)
                value = weighted(value, rw, width).reshape(RING, 2, ROWS, width)
                for k in range(2):
                    Y[p][k, i3, t] = value[:, k]
                return 0

            lax.fori_loop(0, RING, body, 0)
        crossed[p][d] = send(Y[p].at[1 - core, i3], S[p].at[i3], twin)

    def add_twin(p, d):
        i3 = near(ORDER[p][2], d)
        arrived(crossed[p][d], S[p].at[i3])

        def body(i, _):
            Y[p][core, i3, i] = (Y[p][core, i3, i].astype(F32) + S[p][i3, i].astype(F32)).astype(BF)
            return 0

        lax.fori_loop(0, RING, body, 0)

    handed = [{} for _ in range(3)]
    direct = [{} for _ in range(3)]

    def hand_out(p):
        i3 = near(ORDER[p][2], 2)
        for s in (2, 1, 3, 0):
            i2 = near(ORDER[p][1], s)
            for k, o in enumerate((1, 3)):
                handed[p][s, o] = send(sub(p, Y[p].at[core, i3], i2, 2 * k, 2), L[p].at[k, s], peer(ORDER[p][2], o))

    def forward(p, s):
        i2 = near(ORDER[p][1], s)
        for k, o in enumerate((1, 3)):
            i3 = near(ORDER[p][2], o)
            arrived(handed[p][s, o], L[p].at[k, s])
            ref = sub(p, Y[p].at[core, i3], i2, 2 * k, 2)
            ref[...] = (ref[...].astype(F32) + L[p][k, s].astype(F32)).astype(BF)
            direct[p][s, o] = send(sub(p, Y[p].at[core, i3], i2, 0, RING), F[p].at[k, s], peer(ORDER[p][2], o))

    second = [{} for _ in range(3)]
    third_ids = [{} for _ in range(3)]

    def collect(p, s):
        i2 = near(ORDER[p][1], s)
        for k, o in enumerate((1, 3)):
            arrived(direct[p][s, o], F[p].at[k, s])
        value = sub(p, Y[p].at[core, own[p][2]], i2, 0, RING)[...].astype(F32)
        T[p][s] = (value + F[p][0, s].astype(F32) + F[p][1, s].astype(F32)).astype(BF)
        if s:
            second[p][s] = send(T[p].at[s], M[p].at[s - 1], peer(ORDER[p][1], s))

    def collect_line(p):
        value = T[p][0].astype(F32)
        for s in (1, 3, 2):
            arrived(second[p][s], M[p].at[s - 1])
            value = value + M[p][s - 1].astype(F32)
        U[p][...] = value.astype(BF)
        for o in (2, 1, 3):
            third_ids[p][o] = send(U[p].at[near(ORDER[p][0], o)], N[p].at[o - 1], peer(ORDER[p][0], o))

    for p in range(3):
        back(p, 2)
    for p in range(3):
        add_twin(p, 2)
        hand_out(p)
    for d in (1, 3, 0):
        for p in range(3):
            back(p, d)
    for p in range(3):
        add_twin(p, 1)
        add_twin(p, 3)
    for s in (2, 1, 3, 0):
        for p in range(3):
            forward(p, s)
    for p in range(3):
        add_twin(p, 0)
    for s in (2, 1, 3, 0):
        for p in range(3):
            collect(p, s)
    for p in range(3):
        collect_line(p)
    for p in range(3):
        value = U[p][own[p][0]].astype(F32)
        for o in (1, 3, 2):
            arrived(third_ids[p][o], N[p].at[o - 1])
            value = value + N[p][o - 1].astype(F32)
        c = slice(START[p], START[p] + WIDE[p])
        out[:, c] = (hidden[:, c] + value).astype(BF)

    for copy in sends:
        copy.wait_send()


SEMS = 6 + 3 * (3 + 3 + 8 + 8 + 16) + 3 * (4 + 8 + 8 + 3 + 3)


def experts(part, residual, gain, ids, weights, w_gate, w_up, w_down):
    vmem = pl.BlockSpec(memory_space=pltpu.VMEM)
    hbm = pl.BlockSpec(memory_space=pl.ANY)
    V = pltpu.VMEM
    R = RING
    scratch = [
        V((R * SHARE, 2 * HIDDEN), BF),
        V((HIDDEN, R * SHARE), BF),
        V((R, R, R, 2, ROWS, CARRY), BF),
        V((R, R, R, 2, ROWS, CARRY), BF),
        V((R, R, R, 2, ROWS, CARRY), BF),
        V((R, R, 2 * ROWS, 2 * HIDDEN), F32),
        V((R, R, 2 * ROWS, HIDDEN), BF),
        V((R, R, 2 * ROWS, 128), F32),
        V((ROWS, SHARE), F32),
        V((3, ROWS, SHARE), BF),
        V((ROWS, 128), F32),
        V((3, ROWS, 128), F32),
    ]
    scratch += [V((2, R, R, R, ROWS, w), BF) for w in WIDE]
    scratch += [V((R, R, R, ROWS, w), BF) for w in WIDE]
    scratch += [V((2, R, 2, ROWS, w), BF) for w in WIDE]
    scratch += [V((2, R, R, ROWS, w), BF) for w in WIDE]
    scratch += [V((R, R, ROWS, w), BF) for w in WIDE]
    scratch += [V((3, R, ROWS, w), BF) for w in WIDE]
    scratch += [V((R, ROWS, w), BF) for w in WIDE]
    scratch += [V((3, ROWS, w), BF) for w in WIDE]
    scratch += [pltpu.SemaphoreType.DMA((SEMS,)), pltpu.SemaphoreType.DMA((SEMS,)), pltpu.SemaphoreType.DMA((3,))]
    return pl.pallas_call(
        experts_kernel,
        out_shape=jax.ShapeDtypeStruct((ROWS, SHARE), BF),
        in_specs=[vmem] * 5 + [hbm] * 3,
        out_specs=vmem,
        scratch_shapes=scratch,
        compiler_params=pltpu.CompilerParams(
            collective_id=0, has_side_effects=True, vmem_limit_bytes=56 * 1024 * 1024
        ),
    )(part, residual, gain, ids, weights, w_gate, w_up, w_down)


def local(
    query, kv_pool, page_table, lengths, residual, w_out, norm_gain,
    route_ids, route_weights, w_gate, w_up, w_down,
):
    row_count = query.shape[0]
    kv_local = kv_pool.shape[1]
    page_len = kv_pool.shape[3]
    head_dim = kv_pool.shape[4]
    group_size = query.shape[1] // (kv_local * head_dim)
    context = page_table.shape[1] * page_len
    cache = jnp.take(kv_pool, page_table.reshape(-1), axis=2)
    cache = cache.reshape(2, kv_local, row_count, context, head_dim)
    queries = query.reshape(row_count, kv_local, group_size, head_dim)
    scores = jnp.einsum("rkgd,krcd->rkgc", queries, cache[0], preferred_element_type=jnp.float32)
    scores = scores * head_dim ** (-0.5)
    valid_keys = jnp.arange(context, dtype=jnp.int32)[None, :] < lengths[:, None]
    scores = jnp.where(valid_keys[:, None, None, :], scores, -1e30)
    top_score = jnp.max(scores, axis=-1, keepdims=True)
    weights = jnp.exp(scores - top_score)
    probs = (weights / jnp.sum(weights, axis=-1, keepdims=True)).astype(jnp.bfloat16)
    mixed = jnp.einsum("rkgc,krcd->rkgd", probs, cache[1], preferred_element_type=jnp.float32)
    attn = mixed.reshape(row_count, kv_local * group_size * head_dim).astype(jnp.bfloat16)
    part = jnp.einsum("rf,fts->trs", attn, w_out.reshape(-1, RING, SHARE), preferred_element_type=jnp.float32)
    return experts(
        part.astype(BF), residual, norm_gain.reshape(1, -1), route_ids, route_weights, w_gate, w_up, w_down
    )


def solution(mesh):
    in_specs = (
        P("rep", "tp"),
        P(None, "tp", "rep", None, None),
        P("rep", None),
        P("rep"),
        P("rep", None),
        P("tp", None),
        P(),
        P("rep", None),
        P("rep", None),
        P("rep", None, "tp"),
        P("rep", None, "tp"),
        P("rep", "tp", None),
    )
    out_specs = P("rep", "tp")
    return jax.shard_map(local, mesh=mesh, in_specs=in_specs, out_specs=out_specs, check_vma=False)
```

```python
import functools

import jax
import jax.numpy as jnp
from jax import lax
from jax.experimental import pallas as pl
from jax.experimental.pallas import tpu as pltpu
from jax.sharding import PartitionSpec as P

norm_epsilon = 1e-06
MESH = pl.DeviceIdType.MESH
BF, F32 = jnp.bfloat16, jnp.float32
RING = 4
ROWS = 32
SHARE = 1024
GROUP = 8
HEAD = 128
PAGE = 64
PAGES = 256
CONTEXT = 512
HIDDEN = 384
ORDER = (("x", "y", "z"), ("y", "z", "x"), ("z", "x", "y"))
START = (0, 384, 768)
WIDE = (384, 384, 256)
CARRY = 384


def layer_kernel(
    query, kv, pages, lengths, residual, w_out, gain, ids, weights, w_gate, w_up, w_down, out,
    k_in, v_in, w_proj, queries, scores, mixed, part, gains,
    w_in, w_back, g0, g1, g2, acc, act, row_weight, hidden,
    p_in, sq_out, sq_in, y0, y1, y2, s0, s1, s2, l0, l1, l2, f0, f1, f2,
    t0, t1, t2, m0, m1, m2, u0, u1, u2, n0, n1, n2,
    send_sem, recv_sem, load_sem,
):
    rep, y = lax.axis_index("rep"), lax.axis_index("tp")
    x, z, core = rep // 8, (rep // 2) % 4, rep % 2
    at = {"x": x, "y": y, "z": z}
    G, Y, S = (g0, g1, g2), (y0, y1, y2), (s0, s1, s2)
    L, F, T, M, U, N = (l0, l1, l2), (f0, f1, f2), (t0, t1, t2), (m0, m1, m2), (u0, u1, u2), (n0, n1, n2)

    def near(axis, off):
        return lax.rem(at[axis] + off, RING)

    def peer(axis, off):
        c = dict(at)
        c[axis] = near(axis, off)
        return ((c["x"] * RING + c["z"]) * 2 + core, c["y"])

    own = [tuple(at[a] for a in ORDER[p]) for p in range(3)]
    mine = (g0.at[z, y, x, core], g1.at[x, y, z, core], g2.at[y, x, z, core])
    twin = ((x * RING + z) * 2 + 1 - core, y)

    barrier = pltpu.get_barrier_semaphore()
    others = [peer(a, o) for a in "xyz" for o in (1, 2, 3)] + [twin]
    for other in others:
        pl.semaphore_signal(barrier, inc=1, device_id=other, device_id_type=MESH)

    loads = []
    for i, (src, dst) in enumerate((
        (kv.at[0, 0], k_in),
        (kv.at[1, 0], v_in),
        (w_out, w_proj),
        (w_gate.at[0], w_in.at[:, pl.ds(0, HIDDEN)]),
        (w_up.at[0], w_in.at[:, pl.ds(HIDDEN, HIDDEN)]),
        (w_down.at[0], w_back),
    )):
        load = pltpu.make_async_copy(src, dst, load_sem.at[i])
        load.start()
        loads.append(load)

    sends = []

    def send(src, dst, to):
        i = len(sends)
        copy = pltpu.make_async_remote_copy(
            src_ref=src, dst_ref=dst, send_sem=send_sem.at[i], recv_sem=recv_sem.at[i],
            device_id=to, device_id_type=MESH,
        )
        copy.start()
        sends.append(copy)
        return i

    def arrived(i, landing):
        pltpu.make_async_remote_copy(
            src_ref=landing, dst_ref=landing, send_sem=send_sem.at[i], recv_sem=recv_sem.at[i],
            device_id=twin, device_id_type=MESH,
        ).wait_recv()

    for h in range(GROUP):
        queries[h * ROWS : (h + 1) * ROWS, :] = query[:, h * HEAD : (h + 1) * HEAD].astype(F32)
    position = lax.broadcasted_iota(jnp.int32, (GROUP, CONTEXT), 1)

    place = lax.broadcasted_iota(jnp.int32, (128, ROWS), 0)
    spread = jnp.zeros((128, ROWS), F32)
    for k in range(8):
        spread = spread + jnp.where(place % 32 == ids[k : k + 1, :], weights[k : k + 1, :], 0.0)
    top = spread.astype(BF).astype(F32)
    mid = (spread - top).astype(BF).astype(F32)
    low = spread - top - mid
    third = place // 32
    spread = jnp.where(third == 0, top, jnp.where(third == 1, mid, jnp.where(third == 2, low, 0.0)))
    unit = jnp.where(
        lax.broadcasted_iota(jnp.int32, (ROWS, ROWS), 0) == lax.broadcasted_iota(jnp.int32, (ROWS, ROWS), 1), 1.0, 0.0
    ).astype(BF)
    spread = lax.dot_general(unit, spread.astype(BF), (((1,), (1,)), ((), ())), preferred_element_type=F32)
    mine[2][:, WIDE[2] :] = spread.astype(BF)
    gains[...] = gain[...].astype(F32)

    def row_pages(store, b):
        return jnp.concatenate([store[pages[j, b]] for j in range(CONTEXT // PAGE)], axis=0)

    def score(b, _):
        q = queries[pl.ds(b, GROUP, stride=ROWS), :].astype(BF)
        s = lax.dot_general(q, row_pages(k_in, b), (((1,), (1,)), ((), ())), preferred_element_type=F32)
        s = jnp.where(position < lengths[b], s * HEAD ** -0.5, -1e30)
        scores[pl.ds(pl.multiple_of(b * GROUP, GROUP), GROUP), :] = s
        return 0

    def mix(b, _):
        p = scores[pl.ds(pl.multiple_of(b * GROUP, GROUP), GROUP), :].astype(BF)
        mixed[pl.ds(b, GROUP, stride=ROWS), :] = jnp.dot(p, row_pages(v_in, b), preferred_element_type=F32)
        return 0

    loads[0].wait()
    lax.fori_loop(0, ROWS, score, 0, unroll=4)
    s = scores[...]
    s = jnp.exp(s - jnp.max(s, axis=1, keepdims=True))
    scores[...] = s / jnp.sum(s, axis=1, keepdims=True)
    loads[1].wait()
    lax.fori_loop(0, ROWS, mix, 0, unroll=4)
    attn = jnp.concatenate([mixed[h * ROWS : (h + 1) * ROWS, :].astype(BF) for h in range(GROUP)], axis=1)
    loads[2].wait()

    def term(t):
        w = w_proj[:, pl.ds(pl.multiple_of(t * SHARE, SHARE), SHARE)]
        return jnp.dot(attn, w, preferred_element_type=F32)

    ids_p = {}
    for o in (2, 1, 3):
        part[o - 1] = term(near("y", o)).astype(BF)
        if o == 2:
            pl.semaphore_wait(barrier, len(others))
        ids_p[o] = send(part.at[o - 1], p_in.at[o - 1], peer("y", o))
    acc[...] = jnp.zeros_like(acc)
    col = pl.ds(pl.multiple_of(y * SHARE, SHARE), SHARE)
    total = residual[:, col].astype(F32) + term(y)
    for o in (1, 3, 2):
        arrived(ids_p[o], p_in.at[o - 1])
        total = total + p_in[o - 1].astype(F32)
    hidden[...] = total
    square = jnp.sum(total * total, axis=1, keepdims=True)
    sq_out[...] = jnp.broadcast_to(square, (ROWS, 128))
    ids_q = {o: send(sq_out, sq_in.at[o - 1], peer("y", o)) for o in (2, 1, 3)}
    square = sq_out[...]
    for o in (1, 3, 2):
        arrived(ids_q[o], sq_in.at[o - 1])
        square = square + sq_in[o - 1]
    scale = lax.rsqrt(square[:, 0:1] * (1.0 / (RING * SHARE)) + norm_epsilon)
    own_gain = jnp.concatenate(
        [gains[pl.ds(y * (SHARE // 128) + j, 1), :] for j in range(SHARE // 128)], axis=1
    )
    normed = (hidden[...] * scale * own_gain).astype(BF)

    def block(p, i3, i2, first, count, c):
        inner = pl.ds(first, count)
        if p == 1:
            return G[p].at[i3, inner, i2, c]
        return G[p].at[i3, i2, inner, c]

    for p in range(3):
        mine[p][:, 0 : WIDE[p]] = normed[:, START[p] : START[p] + WIDE[p]]

    one = [{} for _ in range(3)]
    two = [{} for _ in range(3)]
    plain = [{} for _ in range(3)]
    relay = [{} for _ in range(3)]
    across = [{} for _ in range(3)]

    def to_twin(p, i3, i2, key):
        ref = block(p, i3, i2, 0, RING, core)
        across[p][key] = send(ref, ref, twin)

    def send_plain(p, s):
        q1, q2, q3 = own[p]
        ref = block(p, q3, near(ORDER[p][1], (4 - s) % 4), 0, RING, core)
        for o in (1, 3):
            plain[p][s, o] = send(ref, ref, peer(ORDER[p][2], o))
        to_twin(p, q3, near(ORDER[p][1], (4 - s) % 4), (0, s))

    for p in range(3):
        q1, q2, q3 = own[p]
        ref = block(p, q3, q2, q1, 1, core)
        for o in (1, 3, 2):
            one[p][o] = send(ref, ref, peer(ORDER[p][0], o))
    for p in range(3):
        q1, q2, q3 = own[p]
        for o in (1, 3, 2):
            arrived(one[p][o], block(p, q3, q2, near(ORDER[p][0], 4 - o), 1, core))
        ref = block(p, q3, q2, 0, RING, core)
        for o in (1, 3, 2):
            two[p][o] = send(ref, ref, peer(ORDER[p][1], o))
        send_plain(p, 0)
    for o in (1, 3, 2):
        for p in range(3):
            q1, q2, q3 = own[p]
            arrived(two[p][o], block(p, q3, near(ORDER[p][1], 4 - o), 0, RING, core))
            send_plain(p, o)

    def pass_on(s):
        for p in range(3):
            i2 = near(ORDER[p][1], (4 - s) % 4)
            for o in (1, 3):
                i3 = near(ORDER[p][2], 4 - o)
                arrived(plain[p][s, o], block(p, i3, i2, 0, RING, core))
                ref = block(p, i3, i2, 0 if o == 1 else 2, 2, core)
                relay[p][s, o] = send(ref, ref, peer(ORDER[p][2], o))
                to_twin(p, i3, i2, (o, s))

    def last_in(s):
        for p in range(3):
            i2 = near(ORDER[p][1], (4 - s) % 4)
            i3 = near(ORDER[p][2], 2)
            arrived(relay[p][s, 1], block(p, i3, i2, 0, 2, core))
            arrived(relay[p][s, 3], block(p, i3, i2, 2, 2, core))
            to_twin(p, i3, i2, (2, s))

    def twin_in(p, d):
        i3 = near(ORDER[p][2], (4 - d) % 4)
        for s in (0, 1, 3, 2):
            i2 = near(ORDER[p][1], (4 - s) % 4)
            arrived(across[p][d, s], block(p, i3, i2, 0, RING, 1 - core))
        return i3

    def project(p, d):
        i3 = twin_in(p, d)
        width = WIDE[p]

        def columns(n, _):
            c = pl.ds(pl.multiple_of(n * 256, 256), 256)
            if p == 2:
                w = w_in[pl.ds(pl.multiple_of(i3 * SHARE + START[2], 256), width), c]
                for i in range(RING):
                    rows = g2[i3, i, :, :, :, 0:width].reshape(256, width)
                    acc[i, :, :, c] += jnp.dot(rows, w, preferred_element_type=F32).reshape(RING, 64, 256)
                return 0
            total = jnp.zeros((256, 256), F32)
            for t in range(RING):
                rows = G[p][i3, t].reshape(256, width)
                w = w_in[t * SHARE + START[p] : t * SHARE + START[p] + width, c]
                total = total + jnp.dot(rows, w, preferred_element_type=F32)
            total = total.reshape(RING, 64, 256)
            if p == 0:
                acc[:, i3, :, c] += total
            else:
                acc[i3, :, :, c] += total
            return 0

        lax.fori_loop(0, 3, columns, 0)

    pass_on(0)
    loads[3].wait()
    loads[4].wait()
    project(0, 0)
    pass_on(1)
    project(1, 0)
    pass_on(3)
    project(2, 0)
    pass_on(2)
    last_in(0)
    project(0, 1)
    project(1, 1)
    last_in(1)
    project(2, 1)
    project(0, 3)
    last_in(3)
    project(1, 3)
    project(2, 3)
    last_in(2)
    for p in range(3):
        project(p, 2)

    pick = lax.broadcasted_iota(jnp.int32, (128, 128), 0)
    pick = jnp.where((pick % 32 == rep) & (pick < 96), 1.0, 0.0).astype(BF)

    def units(i, _):
        table = g2[y, i, :, :, :, 256:384].reshape(256, 128)
        row_weight[i] = jnp.dot(table, pick, preferred_element_type=F32).reshape(RING, 64, 128)
        g = acc[i, :, :, 0:HIDDEN]
        u = acc[i, :, :, HIDDEN : 2 * HIDDEN]
        act[i] = (g / (1.0 + jnp.exp(-g)) * u).astype(BF)
        return 0

    lax.fori_loop(0, RING, units, 0)
    loads[5].wait()

    def sub(p, ref, i2, first, count):
        inner = pl.ds(first, count)
        if p == 1:
            return ref.at[inner, i2]
        return ref.at[i2, inner]

    def weighted(value, w, width):
        return jnp.concatenate(
            [value[:, j * 128 : (j + 1) * 128] * w for j in range(width // 128)], axis=1
        ).astype(BF)

    crossed = [{} for _ in range(3)]

    def back(p, d):
        i3 = near(ORDER[p][2], d)
        width = WIDE[p]
        if p == 2:
            w = w_back[:, pl.ds(pl.multiple_of(i3 * SHARE + START[2], 256), width)]

            def body(i, _):
                value = jnp.dot(act[i].reshape(256, HIDDEN), w, preferred_element_type=F32)
                value = weighted(value, row_weight[i].reshape(256, 128), width).reshape(RING, 2, ROWS, width)
                for k in range(2):
                    y2[k, i3, i] = value[:, k]
                return 0

            lax.fori_loop(0, RING, body, 0)
        else:
            if p == 0:
                a = act[:, i3].reshape(256, HIDDEN)
                rw = row_weight[:, i3].reshape(256, 128)
            else:
                a = act[i3].reshape(256, HIDDEN)
                rw = row_weight[i3].reshape(256, 128)

            def body(t, _):
                w = w_back[:, pl.ds(pl.multiple_of(t * SHARE + START[p], 128), width)]
                value = jnp.dot(a, w, preferred_element_type=F32)
                value = weighted(value, rw, width).reshape(RING, 2, ROWS, width)
                for k in range(2):
                    Y[p][k, i3, t] = value[:, k]
                return 0

            lax.fori_loop(0, RING, body, 0)
        crossed[p][d] = send(Y[p].at[1 - core, i3], S[p].at[i3], twin)

    def add_twin(p, d):
        i3 = near(ORDER[p][2], d)
        arrived(crossed[p][d], S[p].at[i3])

        def body(i, _):
            Y[p][core, i3, i] = (Y[p][core, i3, i].astype(F32) + S[p][i3, i].astype(F32)).astype(BF)
            return 0

        lax.fori_loop(0, RING, body, 0)

    handed = [{} for _ in range(3)]
    direct = [{} for _ in range(3)]

    def hand_out(p):
        i3 = near(ORDER[p][2], 2)
        for s in (2, 1, 3, 0):
            i2 = near(ORDER[p][1], s)
            for k, o in enumerate((1, 3)):
                handed[p][s, o] = send(sub(p, Y[p].at[core, i3], i2, 2 * k, 2), L[p].at[k, s], peer(ORDER[p][2], o))

    def forward(p, s):
        i2 = near(ORDER[p][1], s)
        for k, o in enumerate((1, 3)):
            i3 = near(ORDER[p][2], o)
            arrived(handed[p][s, o], L[p].at[k, s])
            ref = sub(p, Y[p].at[core, i3], i2, 2 * k, 2)
            ref[...] = (ref[...].astype(F32) + L[p][k, s].astype(F32)).astype(BF)
            direct[p][s, o] = send(sub(p, Y[p].at[core, i3], i2, 0, RING), F[p].at[k, s], peer(ORDER[p][2], o))

    second = [{} for _ in range(3)]
    third_ids = [{} for _ in range(3)]

    def collect(p, s):
        i2 = near(ORDER[p][1], s)
        for k, o in enumerate((1, 3)):
            arrived(direct[p][s, o], F[p].at[k, s])
        value = sub(p, Y[p].at[core, own[p][2]], i2, 0, RING)[...].astype(F32)
        T[p][s] = (value + F[p][0, s].astype(F32) + F[p][1, s].astype(F32)).astype(BF)
        if s:
            second[p][s] = send(T[p].at[s], M[p].at[s - 1], peer(ORDER[p][1], s))

    def collect_line(p):
        value = T[p][0].astype(F32)
        for s in (1, 3, 2):
            arrived(second[p][s], M[p].at[s - 1])
            value = value + M[p][s - 1].astype(F32)
        U[p][...] = value.astype(BF)
        for o in (2, 1, 3):
            third_ids[p][o] = send(U[p].at[near(ORDER[p][0], o)], N[p].at[o - 1], peer(ORDER[p][0], o))

    for p in range(3):
        back(p, 2)
    for p in range(3):
        add_twin(p, 2)
        hand_out(p)
    for d in (1, 3, 0):
        for p in range(3):
            back(p, d)
    for p in range(3):
        add_twin(p, 1)
        add_twin(p, 3)
    for s in (2, 1, 3, 0):
        for p in range(3):
            forward(p, s)
    for p in range(3):
        add_twin(p, 0)
    for s in (2, 1, 3, 0):
        for p in range(3):
            collect(p, s)
    for p in range(3):
        collect_line(p)
    for p in range(3):
        value = U[p][own[p][0]].astype(F32)
        for o in (1, 3, 2):
            arrived(third_ids[p][o], N[p].at[o - 1])
            value = value + N[p][o - 1].astype(F32)
        c = slice(START[p], START[p] + WIDE[p])
        out[:, c] = (hidden[:, c] + value).astype(BF)

    for copy in sends:
        copy.wait_send()


SEMS = 6 + 3 * (3 + 3 + 8 + 8 + 16) + 3 * (4 + 8 + 8 + 3 + 3)


def layer(*operands):
    smem = pl.BlockSpec(memory_space=pltpu.SMEM)
    vmem = pl.BlockSpec(memory_space=pltpu.VMEM)
    hbm = pl.BlockSpec(memory_space=pl.ANY)
    V = pltpu.VMEM
    R = RING
    scratch = [
        V((PAGES, PAGE, HEAD), BF),
        V((PAGES, PAGE, HEAD), BF),
        V((SHARE, R * SHARE), BF),
        V((GROUP * ROWS, HEAD), F32),
        V((GROUP * ROWS, CONTEXT), F32),
        V((GROUP * ROWS, HEAD), F32),
        V((3, ROWS, SHARE), BF),
        V((32, 128), F32),
        V((R * SHARE, 2 * HIDDEN), BF),
        V((HIDDEN, R * SHARE), BF),
        V((R, R, R, 2, ROWS, CARRY), BF),
        V((R, R, R, 2, ROWS, CARRY), BF),
        V((R, R, R, 2, ROWS, CARRY), BF),
        V((R, R, 2 * ROWS, 2 * HIDDEN), F32),
        V((R, R, 2 * ROWS, HIDDEN), BF),
        V((R, R, 2 * ROWS, 128), F32),
        V((ROWS, SHARE), F32),
        V((3, ROWS, SHARE), BF),
        V((ROWS, 128), F32),
        V((3, ROWS, 128), F32),
    ]
    scratch += [V((2, R, R, R, ROWS, w), BF) for w in WIDE]
    scratch += [V((R, R, R, ROWS, w), BF) for w in WIDE]
    scratch += [V((2, R, 2, ROWS, w), BF) for w in WIDE]
    scratch += [V((2, R, R, ROWS, w), BF) for w in WIDE]
    scratch += [V((R, R, ROWS, w), BF) for w in WIDE]
    scratch += [V((3, R, ROWS, w), BF) for w in WIDE]
    scratch += [V((R, ROWS, w), BF) for w in WIDE]
    scratch += [V((3, ROWS, w), BF) for w in WIDE]
    scratch += [pltpu.SemaphoreType.DMA((SEMS,)), pltpu.SemaphoreType.DMA((SEMS,)), pltpu.SemaphoreType.DMA((6,))]
    return pl.pallas_call(
        layer_kernel,
        out_shape=jax.ShapeDtypeStruct((ROWS, SHARE), BF),
        in_specs=[vmem, hbm, smem, smem, vmem, hbm] + [vmem] * 3 + [hbm] * 3,
        out_specs=vmem,
        scratch_shapes=scratch,
        compiler_params=pltpu.CompilerParams(
            collective_id=0, has_side_effects=True, vmem_limit_bytes=61 * 1024 * 1024
        ),
    )(*operands)


def local(
    query, kv_pool, page_table, lengths, residual, w_out, norm_gain,
    route_ids, route_weights, w_gate, w_up, w_down,
):
    return layer(
        query, kv_pool, page_table.T, lengths, residual, w_out, norm_gain.reshape(-1, 128),
        route_ids.T, route_weights.T, w_gate, w_up, w_down,
    )


def solution(mesh):
    in_specs = (
        P("rep", "tp"),
        P(None, "tp", "rep", None, None),
        P("rep", None),
        P("rep"),
        P("rep", None),
        P("tp", None),
        P(),
        P("rep", None),
        P("rep", None),
        P("rep", None, "tp"),
        P("rep", None, "tp"),
        P("rep", "tp", None),
    )
    out_specs = P("rep", "tp")
    return jax.shard_map(local, mesh=mesh, in_specs=in_specs, out_specs=out_specs, check_vma=False)
```

```python
import functools

import jax
import jax.numpy as jnp
from jax import lax
from jax.experimental import pallas as pl
from jax.experimental.pallas import tpu as pltpu
from jax.sharding import PartitionSpec as P

norm_epsilon = 1e-06
MESH = pl.DeviceIdType.MESH
BF, F32 = jnp.bfloat16, jnp.float32
RING = 4
ROWS = 32
SHARE = 1024
HALF = 16
MANY = 512
GROUP = 8
HEAD = 128
PAGE = 64
PAGES = 256
CONTEXT = 512
HIDDEN = 384
ORDER = (("x", "y", "z"), ("y", "z", "x"), ("z", "x", "y"))
START = (0, 384, 768)
WIDE = (384, 384, 256)
CARRY = 384


def layer_kernel(
    query, kv, pages, lengths, residual, w_out, gain, ids, weights, w_gate, w_up, w_down, out,
    k_in, v_in, w_proj, queries, scores, mixed, part, gains,
    w_in, w_back, rows, acc, act, row_weight, hidden,
    p_in, sq_out, sq_in, sums, away, crossed, l0, l1, l2, f0, f1, f2,
    t0, t1, t2, m0, m1, m2, u0, u1, u2, n0, n1, n2,
    send_sem, recv_sem, load_sem,
):
    rep, y = lax.axis_index("rep"), lax.axis_index("tp")
    x, z, core = rep // 8, (rep // 2) % 4, rep % 2
    at = {"x": x, "y": y, "z": z}
    L, F, T, M, U, N = (l0, l1, l2), (f0, f1, f2), (t0, t1, t2), (m0, m1, m2), (u0, u1, u2), (n0, n1, n2)

    def near(axis, off):
        return lax.rem(at[axis] + off, RING)

    def peer(axis, off):
        c = dict(at)
        c[axis] = near(axis, off)
        return ((c["x"] * RING + c["z"]) * 2 + core, c["y"])

    twin = ((x * RING + z) * 2 + 1 - core, y)

    barrier = pltpu.get_barrier_semaphore()
    others = [peer(a, o) for a in "xyz" for o in (1, 2, 3)] + [twin]
    for other in others:
        pl.semaphore_signal(barrier, inc=1, device_id=other, device_id_type=MESH)

    loads = []
    for i, (src, dst) in enumerate((
        (kv.at[0, 0], k_in),
        (kv.at[1, 0], v_in),
        (w_out, w_proj),
        (w_gate.at[0], w_in.at[:, pl.ds(0, HIDDEN)]),
        (w_up.at[0], w_in.at[:, pl.ds(HIDDEN, HIDDEN)]),
        (w_down.at[0], w_back),
    )):
        load = pltpu.make_async_copy(src, dst, load_sem.at[i])
        if i < 3:
            load.start()
        loads.append(load)

    sends = []

    def send(src, dst, to):
        i = len(sends)
        copy = pltpu.make_async_remote_copy(
            src_ref=src, dst_ref=dst, send_sem=send_sem.at[i], recv_sem=recv_sem.at[i],
            device_id=to, device_id_type=MESH,
        )
        copy.start()
        sends.append(copy)
        return i

    def arrived(i, landing):
        pltpu.make_async_remote_copy(
            src_ref=landing, dst_ref=landing, send_sem=send_sem.at[i], recv_sem=recv_sem.at[i],
            device_id=twin, device_id_type=MESH,
        ).wait_recv()

    for h in range(GROUP):
        queries[h * ROWS : (h + 1) * ROWS, :] = query[:, h * HEAD : (h + 1) * HEAD].astype(F32)
    position = lax.broadcasted_iota(jnp.int32, (GROUP, CONTEXT), 1)

    place = lax.broadcasted_iota(jnp.int32, (128, ROWS), 0)
    spread = jnp.zeros((128, ROWS), F32)
    for k in range(8):
        spread = spread + jnp.where(place % 32 == ids[k : k + 1, :], weights[k : k + 1, :], 0.0)
    top = spread.astype(BF).astype(F32)
    mid = (spread - top).astype(BF).astype(F32)
    low = spread - top - mid
    third = place // 32
    spread = jnp.where(third == 0, top, jnp.where(third == 1, mid, jnp.where(third == 2, low, 0.0)))
    unit = jnp.where(
        lax.broadcasted_iota(jnp.int32, (ROWS, ROWS), 0) == lax.broadcasted_iota(jnp.int32, (ROWS, ROWS), 1), 1.0, 0.0
    ).astype(BF)
    spread = lax.dot_general(unit, spread.astype(BF), (((1,), (1,)), ((), ())), preferred_element_type=F32)
    for h in range(2):
        rows[h, y, x, z, core, :, SHARE : SHARE + 128] = spread[h * HALF : (h + 1) * HALF].astype(BF)
    gains[...] = gain[...].astype(F32)

    def row_pages(store, b):
        return jnp.concatenate([store[pages[j, b]] for j in range(CONTEXT // PAGE)], axis=0)

    def score(b, _):
        q = queries[pl.ds(b, GROUP, stride=ROWS), :].astype(BF)
        s = lax.dot_general(q, row_pages(k_in, b), (((1,), (1,)), ((), ())), preferred_element_type=F32)
        s = jnp.where(position < lengths[b], s * HEAD ** -0.5, -1e30)
        scores[pl.ds(pl.multiple_of(b * GROUP, GROUP), GROUP), :] = s
        return 0

    def mix(b, _):
        p = scores[pl.ds(pl.multiple_of(b * GROUP, GROUP), GROUP), :].astype(BF)
        mixed[pl.ds(b, GROUP, stride=ROWS), :] = jnp.dot(p, row_pages(v_in, b), preferred_element_type=F32)
        return 0

    loads[0].wait()
    lax.fori_loop(0, ROWS, score, 0, unroll=4)
    s = scores[...]
    s = jnp.exp(s - jnp.max(s, axis=1, keepdims=True))
    scores[...] = s / jnp.sum(s, axis=1, keepdims=True)
    loads[1].wait()
    for load in loads[3:]:
        load.start()
    lax.fori_loop(0, ROWS, mix, 0, unroll=4)
    attn = jnp.concatenate([mixed[h * ROWS : (h + 1) * ROWS, :].astype(BF) for h in range(GROUP)], axis=1)
    loads[2].wait()

    def term(t):
        w = w_proj[:, pl.ds(pl.multiple_of(t * SHARE, SHARE), SHARE)]
        return jnp.dot(attn, w, preferred_element_type=F32)

    ids_p, ids_q = {}, {}
    for o in (2, 1, 3):
        value = term(near("y", o)).astype(BF)
        for h in range(2):
            part[h, o - 1] = value[h * HALF : (h + 1) * HALF]
        if o == 2:
            pl.semaphore_wait(barrier, len(others))
        ids_p[0, o] = send(part.at[0, o - 1], p_in.at[0, o - 1], peer("y", o))
    for o in (2, 1, 3):
        ids_p[1, o] = send(part.at[1, o - 1], p_in.at[1, o - 1], peer("y", o))
    col = pl.ds(pl.multiple_of(y * SHARE, SHARE), SHARE)
    hidden[...] = residual[:, col].astype(F32) + term(y)
    own_gain = jnp.concatenate(
        [gains[pl.ds(y * (SHARE // 128) + j, 1), :] for j in range(SHARE // 128)], axis=1
    )

    def add_terms(h):
        r = slice(h * HALF, (h + 1) * HALF)
        total = hidden[r, :]
        for o in (1, 3, 2):
            arrived(ids_p[h, o], p_in.at[h, o - 1])
            total = total + p_in[h, o - 1].astype(F32)
        hidden[r, :] = total
        sq_out[h] = jnp.broadcast_to(jnp.sum(total * total, axis=1, keepdims=True), (HALF, 128))
        for o in (2, 1, 3):
            ids_q[h, o] = send(sq_out.at[h], sq_in.at[h, o - 1], peer("y", o))

    def normalize(h):
        square = sq_out[h]
        for o in (1, 3, 2):
            arrived(ids_q[h, o], sq_in.at[h, o - 1])
            square = square + sq_in[h, o - 1]
        scale = lax.rsqrt(square[:, 0:1] * (1.0 / (RING * SHARE)) + norm_epsilon)
        value = hidden[h * HALF : (h + 1) * HALF, :] * scale * own_gain
        rows[h, y, x, z, core, :, 0:SHARE] = value.astype(BF)

    def box(p, **sel):
        return tuple(pl.ds(*sel.get(a, (0, RING))) for a in "yxz")

    def named(p, i1=None, i2=None, i3=None):
        return {a: i for a, i in zip(ORDER[p], (i1, i2, i3)) if i is not None}

    def block(p, h, c, i1=None, i2=None, i3=None):
        cols = pl.ds(START[p], CARRY)
        return rows.at[(h,) + box(p, **named(p, i1, i2, i3)) + (c, slice(None), cols)]

    own = [tuple(at[a] for a in ORDER[p]) for p in range(3)]
    ids_g = {}

    def ag1(h):
        for p in range(3):
            q1, q2, q3 = own[p]
            ref = block(p, h, core, (q1, 1), (q2, 1), (q3, 1))
            for o in (1, 3, 2):
                ids_g[1, p, h, o] = send(ref, ref, peer(ORDER[p][0], o))

    def ag2(h):
        for p in range(3):
            q1, q2, q3 = own[p]
            for o in (1, 3, 2):
                arrived(ids_g[1, p, h, o], block(p, h, core, (near(ORDER[p][0], 4 - o), 1), (q2, 1), (q3, 1)))
            ref = block(p, h, core, None, (q2, 1), (q3, 1))
            for o in (1, 3, 2):
                ids_g[2, p, h, o] = send(ref, ref, peer(ORDER[p][1], o))

    def to_twin(p, h, d):
        ref = block(p, h, core, None, None, (near(ORDER[p][2], (4 - d) % 4), 1))
        ids_g["twin", p, h, d] = send(ref, ref, twin)

    def ag3(h):
        for p in range(3):
            q1, q2, q3 = own[p]
            for o in (1, 3, 2):
                arrived(ids_g[2, p, h, o], block(p, h, core, None, (near(ORDER[p][1], 4 - o), 1), (q3, 1)))
            for turn in range(2):
                for k, o in enumerate((1, 3)):
                    ref = block(p, h, core, (2 * ((k + turn) % 2), 2), None, (q3, 1))
                    ids_g[3, p, h, o, turn] = send(ref, ref, peer(ORDER[p][2], o))
        for p in range(3):
            to_twin(p, h, 0)

    def ag4(h):
        for p in range(3):
            for k, o in enumerate((1, 3)):
                ref = block(p, h, core, (2 * k, 2), None, (near(ORDER[p][2], 4 - o), 1))
                arrived(ids_g[3, p, h, o, 0], ref)
                ids_g[4, p, h, o] = send(ref, ref, peer(ORDER[p][2], o))

    def ag5(h):
        for p in range(3):
            for k, o in enumerate((1, 3)):
                arrived(ids_g[3, p, h, o, 1], block(p, h, core, (2 - 2 * k, 2), None, (near(ORDER[p][2], 4 - o), 1)))
                to_twin(p, h, o)

    def ag6(h):
        for p in range(3):
            for k, o in enumerate((1, 3)):
                arrived(ids_g[4, p, h, o], block(p, h, core, (2 * k, 2), None, (near(ORDER[p][2], 2), 1)))
            to_twin(p, h, 2)

    def ag7(h):
        for d in (0, 1, 3, 2):
            for p in range(3):
                ref = block(p, h, 1 - core, None, None, (near(ORDER[p][2], (4 - d) % 4), 1))
                arrived(ids_g["twin", p, h, d], ref)

    pick = lax.broadcasted_iota(jnp.int32, (128, 128), 0)
    pick = jnp.where((pick % 32 == rep) & (pick < 96), 1.0, 0.0).astype(BF)

    def enter(h, *steps):
        for t in steps:
            value = rows[h, t, :, :, :, :, 0:SHARE].reshape(MANY, SHARE)
            value = jnp.dot(value, w_in[t * SHARE : (t + 1) * SHARE, :], preferred_element_type=F32)
            if t == 0:
                acc[...] = value
            else:
                acc[...] += value

    def units(h):
        table = rows[h, y, :, :, :, :, SHARE : SHARE + 128].reshape(MANY, 128)
        weight = jnp.dot(table, pick, preferred_element_type=F32)
        row_weight[...] = weight.reshape(MANY // 32, 2, HALF, 128)
        g = acc[:, 0:HIDDEN]
        u = acc[:, HIDDEN : 2 * HIDDEN]
        act[...] = (g / (1.0 + jnp.exp(-g)) * u).astype(BF).reshape(MANY // 32, 2, HALF, HIDDEN)

    ids_b = {}

    def terms(mine, t):
        w = w_back[:, pl.ds(pl.multiple_of(t * SHARE, SHARE), SHARE)]
        value = jnp.dot(act[:, mine].reshape(MANY // 2, HIDDEN), w, preferred_element_type=F32)
        rw = row_weight[:, mine].reshape(MANY // 2, 128)
        value = jnp.concatenate([value[:, j * 128 : (j + 1) * 128] * rw for j in range(SHARE // 128)], axis=1)
        return value.reshape(RING, RING, HALF, SHARE)

    def leave_twin(h, o):
        t = near("y", o)
        away[h, t] = terms(1 - core, t).astype(BF)
        ids_b["twin", h, o] = send(away.at[h, t], crossed.at[h, t], twin)

    def leave_own(h, o):
        t = near("y", o)
        value = terms(core, t)
        arrived(ids_b["twin", h, o], crossed.at[h, t])
        sums[h, t] = (value + crossed[h, t].astype(F32)).astype(BF)

    def term_of(p, h, i1=None, i2=None, i3=None):
        cols = pl.ds(START[p], WIDE[p])
        return sums.at[(h,) + box(p, **named(p, i1, i2, i3)) + (slice(None), cols)]

    def part_of(ref, lead, p, i1=None, i2=None):
        return ref[p].at[lead + box(p, **named(p, i1, i2, (0, 1)))]

    def rs1(h, pieces):
        for p in pieces:
            axis = ORDER[p][2]
            far = (near(axis, 2), 1)
            for k, o in enumerate((1, 3)):
                ids_b[1, p, h, o] = send(term_of(p, h, (2 * k, 2), None, far), L[p].at[h, k], peer(axis, o))
            for k, o in enumerate((1, 3)):
                ids_b[2, p, h, o, 0] = send(
                    term_of(p, h, (2 - 2 * k, 2), None, (near(axis, o), 1)),
                    part_of(F, (h, k), p, (2 - 2 * k, 2)), peer(axis, o),
                )

    def rs2(h):
        for p in range(3):
            axis = ORDER[p][2]
            for k, o in enumerate((1, 3)):
                arrived(ids_b[1, p, h, o], L[p].at[h, k])
                ref = term_of(p, h, (2 * k, 2), None, (near(axis, o), 1))
                ref[...] = ref[...] + L[p][h, k]
                ids_b[2, p, h, o, 1] = send(ref, part_of(F, (h, k), p, (2 * k, 2)), peer(axis, o))

    def rs3(h):
        for p in range(3):
            for k, o in enumerate((1, 3)):
                arrived(ids_b[2, p, h, o, 0], part_of(F, (h, k), p, (2 - 2 * k, 2)))
                arrived(ids_b[2, p, h, o, 1], part_of(F, (h, k), p, (2 * k, 2)))
            value = term_of(p, h, None, None, (own[p][2], 1))[...].astype(F32)
            T[p][h] = (value + F[p][h, 0].astype(F32) + F[p][h, 1].astype(F32)).astype(BF)
            axis = ORDER[p][1]
            for o in (2, 1, 3):
                ref = part_of(T, (h,), p, None, (near(axis, o), 1))
                ids_b[3, p, h, o] = send(ref, M[p].at[h, o - 1], peer(axis, o))

    def rs4(h):
        for p in range(3):
            value = part_of(T, (h,), p, None, (own[p][1], 1))[...].astype(F32)
            for o in (1, 3, 2):
                arrived(ids_b[3, p, h, o], M[p].at[h, o - 1])
                value = value + M[p][h, o - 1].astype(F32)
            U[p][h] = value.astype(BF).reshape(RING, HALF, WIDE[p])
            for o in (2, 1, 3):
                ids_b[4, p, h, o] = send(U[p].at[h, near(ORDER[p][0], o)], N[p].at[h, o - 1], peer(ORDER[p][0], o))

    def rs5(h):
        r = slice(h * HALF, (h + 1) * HALF)
        for p in range(3):
            value = U[p][h, own[p][0]].astype(F32)
            for o in (1, 3, 2):
                arrived(ids_b[4, p, h, o], N[p].at[h, o - 1])
                value = value + N[p][h, o - 1].astype(F32)
            c = slice(START[p], START[p] + WIDE[p])
            out[r, c] = (hidden[r, c] + value).astype(BF)

    add_terms(0)
    add_terms(1)
    normalize(0)
    ag1(0)
    normalize(1)
    ag1(1)
    ag2(0)
    ag3(0)
    ag2(1)
    ag4(0)
    ag3(1)
    ag5(0)
    ag6(0)
    for load in loads[3:]:
        load.wait()
    ag7(0)
    enter(0, 0)
    ag4(1)
    enter(0, 1, 2)
    ag5(1)
    enter(0, 3)
    units(0)
    for o in (2, 1, 3, 0):
        leave_twin(0, o)
    ag6(1)
    for o in (2, 1, 3):
        leave_own(0, o)
    rs1(0, (2,))
    leave_own(0, 0)
    rs1(0, (0, 1))
    ag7(1)
    enter(1, 0, 1)
    rs2(0)
    enter(1, 2, 3)
    units(1)
    for o in (2, 1, 3, 0):
        leave_twin(1, o)
    rs3(0)
    for o in (2, 1, 3):
        leave_own(1, o)
    rs1(1, (2,))
    leave_own(1, 0)
    rs1(1, (0, 1))
    rs4(0)
    rs2(1)
    rs5(0)
    rs3(1)
    rs4(1)
    rs5(1)

    for copy in sends:
        copy.wait_send()


SEMS = 12 + 2 * 3 * (3 + 3 + 4 + 2 + 4) + 2 * (4 + 3 * (2 + 4 + 3 + 3))


def layer(*operands):
    smem = pl.BlockSpec(memory_space=pltpu.SMEM)
    vmem = pl.BlockSpec(memory_space=pltpu.VMEM)
    hbm = pl.BlockSpec(memory_space=pl.ANY)
    V = pltpu.VMEM
    R = RING
    scratch = [
        V((PAGES, PAGE, HEAD), BF),
        V((PAGES, PAGE, HEAD), BF),
        V((SHARE, R * SHARE), BF),
        V((GROUP * ROWS, HEAD), F32),
        V((GROUP * ROWS, CONTEXT), F32),
        V((GROUP * ROWS, HEAD), F32),
        V((2, 3, HALF, SHARE), BF),
        V((32, 128), F32),
        V((R * SHARE, 2 * HIDDEN), BF),
        V((HIDDEN, R * SHARE), BF),
        V((2, R, R, R, 2, HALF, SHARE + 128), BF),
        V((MANY, 2 * HIDDEN), F32),
        V((MANY // 32, 2, HALF, HIDDEN), BF),
        V((MANY // 32, 2, HALF, 128), F32),
        V((ROWS, SHARE), F32),
        V((2, 3, HALF, SHARE), BF),
        V((2, HALF, 128), F32),
        V((2, 3, HALF, 128), F32),
        V((2, R, R, R, HALF, SHARE), BF),
        V((2, R, R, R, HALF, SHARE), BF),
        V((2, R, R, R, HALF, SHARE), BF),
    ]

    def sizes(p, *cut):
        cut = dict(zip(ORDER[p][::-1], cut))
        return tuple(cut.get(a, R) for a in "yxz") + (HALF, WIDE[p])

    scratch += [V((2, 2) + sizes(p, 1, R, 2), BF) for p in range(3)]
    scratch += [V((2, 2) + sizes(p, 1), BF) for p in range(3)]
    scratch += [V((2,) + sizes(p, 1), BF) for p in range(3)]
    scratch += [V((2, 3) + sizes(p, 1, 1), BF) for p in range(3)]
    scratch += [V((2, R, HALF, w), BF) for w in WIDE]
    scratch += [V((2, 3, HALF, w), BF) for w in WIDE]
    scratch += [pltpu.SemaphoreType.DMA((SEMS,)), pltpu.SemaphoreType.DMA((SEMS,)), pltpu.SemaphoreType.DMA((6,))]
    return pl.pallas_call(
        layer_kernel,
        out_shape=jax.ShapeDtypeStruct((ROWS, SHARE), BF),
        in_specs=[vmem, hbm, smem, smem, vmem, hbm] + [vmem] * 3 + [hbm] * 3,
        out_specs=vmem,
        scratch_shapes=scratch,
        compiler_params=pltpu.CompilerParams(
            collective_id=0, has_side_effects=True, vmem_limit_bytes=61 * 1024 * 1024
        ),
    )(*operands)


def local(
    query, kv_pool, page_table, lengths, residual, w_out, norm_gain,
    route_ids, route_weights, w_gate, w_up, w_down,
):
    return layer(
        query, kv_pool, page_table.T, lengths, residual, w_out, norm_gain.reshape(-1, 128),
        route_ids.T, route_weights.T, w_gate, w_up, w_down,
    )


def solution(mesh):
    in_specs = (
        P("rep", "tp"),
        P(None, "tp", "rep", None, None),
        P("rep", None),
        P("rep"),
        P("rep", None),
        P("tp", None),
        P(),
        P("rep", None),
        P("rep", None),
        P("rep", None, "tp"),
        P("rep", None, "tp"),
        P("rep", "tp", None),
    )
    out_specs = P("rep", "tp")
    return jax.shard_map(local, mesh=mesh, in_specs=in_specs, out_specs=out_specs, check_vma=False)
```

```python
import functools

import jax
import jax.numpy as jnp
from jax import lax
from jax.experimental import pallas as pl
from jax.experimental.pallas import tpu as pltpu
from jax.sharding import PartitionSpec as P

norm_epsilon = 1e-06
MESH = pl.DeviceIdType.MESH
BF, F32 = jnp.bfloat16, jnp.float32
RING = 4
ROWS = 32
SHARE = 1024
EARLY = 16
HALF = 16
MANY = 512
GROUP = 8
HEAD = 128
PAGE = 64
PAGES = 256
CONTEXT = 512
HIDDEN = 384
ORDER = (("x", "y", "z"), ("y", "z", "x"), ("z", "x", "y"))
START = (0, 384, 768)
WIDE = (384, 384, 256)
CARRY = 384


def layer_kernel(
    query, kv, pages, lengths, residual, w_out, gain, ids, weights, w_gate, w_up, w_down, out,
    k_in, v_in, w_proj, queries, scores, mixed, part, gains,
    w_in, w_back, rows, acc, act, row_weight, hidden,
    p_in, sq_out, sq_in, sums, away, crossed, l0, l1, l2, f0, f1, f2,
    t0, t1, t2, m0, m1, m2, u0, u1, u2, n0, n1, n2,
    send_sem, recv_sem, load_sem,
):
    rep, y = lax.axis_index("rep"), lax.axis_index("tp")
    x, z, core = rep // 8, (rep // 2) % 4, rep % 2
    at = {"x": x, "y": y, "z": z}
    L, F, T, M, U, N = (l0, l1, l2), (f0, f1, f2), (t0, t1, t2), (m0, m1, m2), (u0, u1, u2), (n0, n1, n2)

    def near(axis, off):
        return lax.rem(at[axis] + off, RING)

    def peer(axis, off):
        c = dict(at)
        c[axis] = near(axis, off)
        return ((c["x"] * RING + c["z"]) * 2 + core, c["y"])

    twin = ((x * RING + z) * 2 + 1 - core, y)

    barrier = pltpu.get_barrier_semaphore()
    others = [peer(a, o) for a in "xyz" for o in (1, 2, 3)] + [twin]
    for other in others:
        pl.semaphore_signal(barrier, inc=1, device_id=other, device_id_type=MESH)

    loads = []
    for i, (src, dst) in enumerate((
        *[(kv.at[0, 0, pl.ds(i * 64, 64)], k_in.at[pl.ds(i * 64, 64)]) for i in range(4)],
        *[(kv.at[1, 0, pl.ds(i * 64, 64)], v_in.at[pl.ds(i * 64, 64)]) for i in range(4)],
        *[(w_out.at[pl.ds(i * 128, 128)], w_proj.at[pl.ds(i * 128, 128)]) for i in range(8)],
        (w_gate.at[0], w_in.at[:, pl.ds(0, HIDDEN)]),
        (w_up.at[0], w_in.at[:, pl.ds(HIDDEN, HIDDEN)]),
        (w_down.at[0], w_back),
    )):
        load = pltpu.make_async_copy(src, dst, load_sem.at[i])
        if i < EARLY:
            load.start()
        loads.append(load)

    sends = []

    def send(src, dst, to):
        i = len(sends)
        copy = pltpu.make_async_remote_copy(
            src_ref=src, dst_ref=dst, send_sem=send_sem.at[i], recv_sem=recv_sem.at[i],
            device_id=to, device_id_type=MESH,
        )
        copy.start()
        sends.append(copy)
        return i

    def arrived(i, landing):
        pltpu.make_async_remote_copy(
            src_ref=landing, dst_ref=landing, send_sem=send_sem.at[i], recv_sem=recv_sem.at[i],
            device_id=twin, device_id_type=MESH,
        ).wait_recv()

    for h in range(GROUP):
        queries[h * ROWS : (h + 1) * ROWS, :] = query[:, h * HEAD : (h + 1) * HEAD].astype(F32)
    position = lax.broadcasted_iota(jnp.int32, (GROUP, CONTEXT), 1)

    place = lax.broadcasted_iota(jnp.int32, (128, ROWS), 0)
    spread = jnp.zeros((128, ROWS), F32)
    for k in range(8):
        spread = spread + jnp.where(place % 32 == ids[k : k + 1, :], weights[k : k + 1, :], 0.0)
    top = spread.astype(BF).astype(F32)
    mid = (spread - top).astype(BF).astype(F32)
    low = spread - top - mid
    third = place // 32
    spread = jnp.where(third == 0, top, jnp.where(third == 1, mid, jnp.where(third == 2, low, 0.0)))
    unit = jnp.where(
        lax.broadcasted_iota(jnp.int32, (ROWS, ROWS), 0) == lax.broadcasted_iota(jnp.int32, (ROWS, ROWS), 1), 1.0, 0.0
    ).astype(BF)
    spread = lax.dot_general(unit, spread.astype(BF), (((1,), (1,)), ((), ())), preferred_element_type=F32)
    for h in range(2):
        rows[h, y, x, z, core, :, SHARE : SHARE + 128] = spread[h * HALF : (h + 1) * HALF].astype(BF)
    gains[...] = gain[...].astype(F32)

    def row_pages(store, b):
        return jnp.concatenate([store[pages[j, b]] for j in range(CONTEXT // PAGE)], axis=0)

    def score(b, _):
        q = queries[pl.ds(b, GROUP, stride=ROWS), :].astype(BF)
        s = lax.dot_general(q, row_pages(k_in, b), (((1,), (1,)), ((), ())), preferred_element_type=F32)
        s = jnp.where(position < lengths[b], s * HEAD ** -0.5, -1e30)
        scores[pl.ds(pl.multiple_of(b * GROUP, GROUP), GROUP), :] = s
        return 0

    def mix(b, _):
        p = scores[pl.ds(pl.multiple_of(b * GROUP, GROUP), GROUP), :].astype(BF)
        mixed[pl.ds(b, GROUP, stride=ROWS), :] = jnp.dot(p, row_pages(v_in, b), preferred_element_type=F32)
        return 0

    for load in loads[0:4]:
        load.wait()
    lax.fori_loop(0, ROWS, score, 0, unroll=4)
    s = scores[...]
    s = jnp.exp(s - jnp.max(s, axis=1, keepdims=True))
    scores[...] = s / jnp.sum(s, axis=1, keepdims=True)
    for load in loads[4:8]:
        load.wait()
    for load in loads[EARLY:]:
        load.start()
    lax.fori_loop(0, ROWS, mix, 0, unroll=4)
    attn = jnp.concatenate([mixed[h * ROWS : (h + 1) * ROWS, :].astype(BF) for h in range(GROUP)], axis=1)
    for load in loads[8:EARLY]:
        load.wait()

    def term(t):
        w = w_proj[:, pl.ds(pl.multiple_of(t * SHARE, SHARE), SHARE)]
        return jnp.dot(attn, w, preferred_element_type=F32)

    ids_p, ids_q = {}, {}
    for o in (2, 1, 3):
        value = term(near("y", o)).astype(BF)
        for h in range(2):
            part[h, o - 1] = value[h * HALF : (h + 1) * HALF]
        if o == 2:
            pl.semaphore_wait(barrier, len(others))
        ids_p[0, o] = send(part.at[0, o - 1], p_in.at[0, o - 1], peer("y", o))
    for o in (2, 1, 3):
        ids_p[1, o] = send(part.at[1, o - 1], p_in.at[1, o - 1], peer("y", o))
    col = pl.ds(pl.multiple_of(y * SHARE, SHARE), SHARE)
    hidden[...] = residual[:, col].astype(F32) + term(y)
    own_gain = jnp.concatenate(
        [gains[pl.ds(y * (SHARE // 128) + j, 1), :] for j in range(SHARE // 128)], axis=1
    )

    def add_terms(h):
        r = slice(h * HALF, (h + 1) * HALF)
        total = hidden[r, :]
        for o in (1, 3, 2):
            arrived(ids_p[h, o], p_in.at[h, o - 1])
            total = total + p_in[h, o - 1].astype(F32)
        hidden[r, :] = total
        sq_out[h] = jnp.broadcast_to(jnp.sum(total * total, axis=1, keepdims=True), (HALF, 128))
        for o in (2, 1, 3):
            ids_q[h, o] = send(sq_out.at[h], sq_in.at[h, o - 1], peer("y", o))

    def normalize(h):
        square = sq_out[h]
        for o in (1, 3, 2):
            arrived(ids_q[h, o], sq_in.at[h, o - 1])
            square = square + sq_in[h, o - 1]
        scale = lax.rsqrt(square[:, 0:1] * (1.0 / (RING * SHARE)) + norm_epsilon)
        value = hidden[h * HALF : (h + 1) * HALF, :] * scale * own_gain
        rows[h, y, x, z, core, :, 0:SHARE] = value.astype(BF)

    def box(p, **sel):
        return tuple(pl.ds(*sel.get(a, (0, RING))) for a in "yxz")

    def named(p, i1=None, i2=None, i3=None):
        return {a: i for a, i in zip(ORDER[p], (i1, i2, i3)) if i is not None}

    def block(p, h, c, i1=None, i2=None, i3=None):
        cols = pl.ds(START[p], CARRY)
        return rows.at[(h,) + box(p, **named(p, i1, i2, i3)) + (c, slice(None), cols)]

    own = [tuple(at[a] for a in ORDER[p]) for p in range(3)]
    ids_g = {}

    def ag1(h):
        for p in range(3):
            q1, q2, q3 = own[p]
            ref = block(p, h, core, (q1, 1), (q2, 1), (q3, 1))
            for o in (1, 3, 2):
                ids_g[1, p, h, o] = send(ref, ref, peer(ORDER[p][0], o))

    def ag2(h):
        for p in range(3):
            q1, q2, q3 = own[p]
            for o in (1, 3, 2):
                arrived(ids_g[1, p, h, o], block(p, h, core, (near(ORDER[p][0], 4 - o), 1), (q2, 1), (q3, 1)))
            ref = block(p, h, core, None, (q2, 1), (q3, 1))
            for o in (1, 3, 2):
                ids_g[2, p, h, o] = send(ref, ref, peer(ORDER[p][1], o))

    def to_twin(p, h, d):
        ref = block(p, h, core, None, None, (near(ORDER[p][2], (4 - d) % 4), 1))
        ids_g["twin", p, h, d] = send(ref, ref, twin)

    def ag3(h):
        for p in range(3):
            q1, q2, q3 = own[p]
            for o in (1, 3, 2):
                arrived(ids_g[2, p, h, o], block(p, h, core, None, (near(ORDER[p][1], 4 - o), 1), (q3, 1)))
            for turn in range(2):
                for k, o in enumerate((1, 3)):
                    ref = block(p, h, core, (2 * ((k + turn) % 2), 2), None, (q3, 1))
                    ids_g[3, p, h, o, turn] = send(ref, ref, peer(ORDER[p][2], o))
        for p in range(3):
            to_twin(p, h, 0)

    def ag4(h):
        for p in range(3):
            for k, o in enumerate((1, 3)):
                ref = block(p, h, core, (2 * k, 2), None, (near(ORDER[p][2], 4 - o), 1))
                arrived(ids_g[3, p, h, o, 0], ref)
                ids_g[4, p, h, o] = send(ref, ref, peer(ORDER[p][2], o))

    def ag5(h):
        for p in range(3):
            for k, o in enumerate((1, 3)):
                arrived(ids_g[3, p, h, o, 1], block(p, h, core, (2 - 2 * k, 2), None, (near(ORDER[p][2], 4 - o), 1)))
                to_twin(p, h, o)

    def ag6(h):
        for p in range(3):
            for k, o in enumerate((1, 3)):
                arrived(ids_g[4, p, h, o], block(p, h, core, (2 * k, 2), None, (near(ORDER[p][2], 2), 1)))
            to_twin(p, h, 2)

    def ag7(h):
        for d in (0, 1, 3, 2):
            for p in range(3):
                ref = block(p, h, 1 - core, None, None, (near(ORDER[p][2], (4 - d) % 4), 1))
                arrived(ids_g["twin", p, h, d], ref)

    pick = lax.broadcasted_iota(jnp.int32, (128, 128), 0)
    pick = jnp.where((pick % 32 == rep) & (pick < 96), 1.0, 0.0).astype(BF)

    def enter(h, *steps):
        for t in steps:
            value = rows[h, t, :, :, :, :, 0:SHARE].reshape(MANY, SHARE)
            value = jnp.dot(value, w_in[t * SHARE : (t + 1) * SHARE, :], preferred_element_type=F32)
            if t == 0:
                acc[...] = value
            else:
                acc[...] += value

    def units(h):
        table = rows[h, y, :, :, :, :, SHARE : SHARE + 128].reshape(MANY, 128)
        weight = jnp.dot(table, pick, preferred_element_type=F32)
        row_weight[...] = weight.reshape(MANY // 32, 2, HALF, 128)
        g = acc[:, 0:HIDDEN]
        u = acc[:, HIDDEN : 2 * HIDDEN]
        act[...] = (g / (1.0 + jnp.exp(-g)) * u).astype(BF).reshape(MANY // 32, 2, HALF, HIDDEN)

    ids_b = {}

    def terms(mine, t):
        w = w_back[:, pl.ds(pl.multiple_of(t * SHARE, SHARE), SHARE)]
        value = jnp.dot(act[:, mine].reshape(MANY // 2, HIDDEN), w, preferred_element_type=F32)
        rw = row_weight[:, mine].reshape(MANY // 2, 128)
        value = jnp.concatenate([value[:, j * 128 : (j + 1) * 128] * rw for j in range(SHARE // 128)], axis=1)
        return value.reshape(RING, RING, HALF, SHARE)

    def leave_twin(h, o):
        t = near("y", o)
        away[h, t] = terms(1 - core, t).astype(BF)
        ids_b["twin", h, o] = send(away.at[h, t], crossed.at[h, t], twin)

    def leave_own(h, o):
        t = near("y", o)
        value = terms(core, t)
        arrived(ids_b["twin", h, o], crossed.at[h, t])
        sums[h, t] = (value + crossed[h, t].astype(F32)).astype(BF)

    def term_of(p, h, i1=None, i2=None, i3=None):
        cols = pl.ds(START[p], WIDE[p])
        return sums.at[(h,) + box(p, **named(p, i1, i2, i3)) + (slice(None), cols)]

    def part_of(ref, lead, p, i1=None, i2=None):
        return ref[p].at[lead + box(p, **named(p, i1, i2, (0, 1)))]

    def rs1(h, pieces):
        for p in pieces:
            axis = ORDER[p][2]
            far = (near(axis, 2), 1)
            for k, o in enumerate((1, 3)):
                ids_b[1, p, h, o] = send(term_of(p, h, (2 * k, 2), None, far), L[p].at[h, k], peer(axis, o))
            for k, o in enumerate((1, 3)):
                ids_b[2, p, h, o, 0] = send(
                    term_of(p, h, (2 - 2 * k, 2), None, (near(axis, o), 1)),
                    part_of(F, (h, k), p, (2 - 2 * k, 2)), peer(axis, o),
                )

    def rs2(h):
        for p in range(3):
            axis = ORDER[p][2]
            for k, o in enumerate((1, 3)):
                arrived(ids_b[1, p, h, o], L[p].at[h, k])
                ref = term_of(p, h, (2 * k, 2), None, (near(axis, o), 1))
                ref[...] = ref[...] + L[p][h, k]
                ids_b[2, p, h, o, 1] = send(ref, part_of(F, (h, k), p, (2 * k, 2)), peer(axis, o))

    def rs3(h):
        for p in range(3):
            for k, o in enumerate((1, 3)):
                arrived(ids_b[2, p, h, o, 0], part_of(F, (h, k), p, (2 - 2 * k, 2)))
                arrived(ids_b[2, p, h, o, 1], part_of(F, (h, k), p, (2 * k, 2)))
            value = term_of(p, h, None, None, (own[p][2], 1))[...].astype(F32)
            T[p][h] = (value + F[p][h, 0].astype(F32) + F[p][h, 1].astype(F32)).astype(BF)
            axis = ORDER[p][1]
            for o in (2, 1, 3):
                ref = part_of(T, (h,), p, None, (near(axis, o), 1))
                ids_b[3, p, h, o] = send(ref, M[p].at[h, o - 1], peer(axis, o))

    def rs4(h):
        for p in range(3):
            value = part_of(T, (h,), p, None, (own[p][1], 1))[...].astype(F32)
            for o in (1, 3, 2):
                arrived(ids_b[3, p, h, o], M[p].at[h, o - 1])
                value = value + M[p][h, o - 1].astype(F32)
            U[p][h] = value.astype(BF).reshape(RING, HALF, WIDE[p])
            for o in (2, 1, 3):
                ids_b[4, p, h, o] = send(U[p].at[h, near(ORDER[p][0], o)], N[p].at[h, o - 1], peer(ORDER[p][0], o))

    def rs5(h):
        r = slice(h * HALF, (h + 1) * HALF)
        for p in range(3):
            value = U[p][h, own[p][0]].astype(F32)
            for o in (1, 3, 2):
                arrived(ids_b[4, p, h, o], N[p].at[h, o - 1])
                value = value + N[p][h, o - 1].astype(F32)
            c = slice(START[p], START[p] + WIDE[p])
            out[r, c] = (hidden[r, c] + value).astype(BF)

    add_terms(0)
    add_terms(1)
    normalize(0)
    ag1(0)
    normalize(1)
    ag1(1)
    ag2(0)
    ag2(1)
    ag3(0)
    ag3(1)
    ag4(0)
    ag5(0)
    ag6(0)
    for load in loads[EARLY:]:
        load.wait()
    ag7(0)
    enter(0, 0)
    ag4(1)
    enter(0, 1, 2)
    ag5(1)
    enter(0, 3)
    units(0)
    for o in (2, 1, 3, 0):
        leave_twin(0, o)
    ag6(1)
    for o in (2, 1, 3):
        leave_own(0, o)
    rs1(0, (2,))
    leave_own(0, 0)
    rs1(0, (0, 1))
    ag7(1)
    enter(1, 0, 1)
    rs2(0)
    enter(1, 2, 3)
    units(1)
    for o in (2, 1, 3, 0):
        leave_twin(1, o)
    rs3(0)
    for o in (2, 1, 3):
        leave_own(1, o)
    rs1(1, (2,))
    leave_own(1, 0)
    rs1(1, (0, 1))
    rs4(0)
    rs2(1)
    rs5(0)
    rs3(1)
    rs4(1)
    rs5(1)

    for copy in sends:
        copy.wait_send()


SEMS = 12 + 2 * 3 * (3 + 3 + 4 + 2 + 4) + 2 * (4 + 3 * (2 + 4 + 3 + 3))


def layer(*operands):
    smem = pl.BlockSpec(memory_space=pltpu.SMEM)
    vmem = pl.BlockSpec(memory_space=pltpu.VMEM)
    hbm = pl.BlockSpec(memory_space=pl.ANY)
    V = pltpu.VMEM
    R = RING
    scratch = [
        V((PAGES, PAGE, HEAD), BF),
        V((PAGES, PAGE, HEAD), BF),
        V((SHARE, R * SHARE), BF),
        V((GROUP * ROWS, HEAD), F32),
        V((GROUP * ROWS, CONTEXT), F32),
        V((GROUP * ROWS, HEAD), F32),
        V((2, 3, HALF, SHARE), BF),
        V((32, 128), F32),
        V((R * SHARE, 2 * HIDDEN), BF),
        V((HIDDEN, R * SHARE), BF),
        V((2, R, R, R, 2, HALF, SHARE + 128), BF),
        V((MANY, 2 * HIDDEN), F32),
        V((MANY // 32, 2, HALF, HIDDEN), BF),
        V((MANY // 32, 2, HALF, 128), F32),
        V((ROWS, SHARE), F32),
        V((2, 3, HALF, SHARE), BF),
        V((2, HALF, 128), F32),
        V((2, 3, HALF, 128), F32),
        V((2, R, R, R, HALF, SHARE), BF),
        V((2, R, R, R, HALF, SHARE), BF),
        V((2, R, R, R, HALF, SHARE), BF),
    ]

    def sizes(p, *cut):
        cut = dict(zip(ORDER[p][::-1], cut))
        return tuple(cut.get(a, R) for a in "yxz") + (HALF, WIDE[p])

    scratch += [V((2, 2) + sizes(p, 1, R, 2), BF) for p in range(3)]
    scratch += [V((2, 2) + sizes(p, 1), BF) for p in range(3)]
    scratch += [V((2,) + sizes(p, 1), BF) for p in range(3)]
    scratch += [V((2, 3) + sizes(p, 1, 1), BF) for p in range(3)]
    scratch += [V((2, R, HALF, w), BF) for w in WIDE]
    scratch += [V((2, 3, HALF, w), BF) for w in WIDE]
    scratch += [pltpu.SemaphoreType.DMA((SEMS,)), pltpu.SemaphoreType.DMA((SEMS,)), pltpu.SemaphoreType.DMA((EARLY + 3,))]
    return pl.pallas_call(
        layer_kernel,
        out_shape=jax.ShapeDtypeStruct((ROWS, SHARE), BF),
        in_specs=[vmem, hbm, smem, smem, vmem, hbm] + [vmem] * 3 + [hbm] * 3,
        out_specs=vmem,
        scratch_shapes=scratch,
        compiler_params=pltpu.CompilerParams(
            collective_id=0, has_side_effects=True, vmem_limit_bytes=61 * 1024 * 1024
        ),
    )(*operands)


def local(
    query, kv_pool, page_table, lengths, residual, w_out, norm_gain,
    route_ids, route_weights, w_gate, w_up, w_down,
):
    return layer(
        query, kv_pool, page_table.T, lengths, residual, w_out, norm_gain.reshape(-1, 128),
        route_ids.T, route_weights.T, w_gate, w_up, w_down,
    )


def solution(mesh):
    in_specs = (
        P("rep", "tp"),
        P(None, "tp", "rep", None, None),
        P("rep", None),
        P("rep"),
        P("rep", None),
        P("tp", None),
        P(),
        P("rep", None),
        P("rep", None),
        P("rep", None, "tp"),
        P("rep", None, "tp"),
        P("rep", "tp", None),
    )
    out_specs = P("rep", "tp")
    return jax.shard_map(local, mesh=mesh, in_specs=in_specs, out_specs=out_specs, check_vma=False)
```
